256 devices in a mesh: ta: 16 (over z_lo, y, core), gz: 16 (over x, z_hi).
Axes of the slice: x: 4, y: 4, z: 8 (z_hi: 4, z_lo: 2; z = z_hi * 2 + z_lo), core: 2. Of those that a mesh axis runs over, the one named last changes fastest.
Arguments:
- source: bfloat16 [16, 16, 16, 96, 128], P('ta', 'gz'), may hold values from -6 to 6
- link_blocks: bfloat16 [16, 16, 16, 9, 96, 96], P('ta', 'gz'), may hold values from -0.21875 to 0.21875
Outputs:
- result: float32 [16, 16, 16, 96, 128], P('ta', 'gz')
The draws below stay inside these ranges and needn't reach their ends.
All inputs are finite; a program needn't handle non-finite values.
Results may differ from the reference program's by a relative error of at most 0.0049.
Values may be sent and summed in bfloat16 or wider, within the bound.
A program may use at most 64 MiB of HBM per device.

```python
import jax
import jax.numpy as jnp
from jax import lax

DOF = 96
DIRS = 9
RHS = 128
NX = 8
NY = 2
APPLIES = 4
NYX = 16
NT = 16
NZ = 16


def block_levels(stream_key, dims, split, smallest, high):
    loudness = 1.0
    for position, parts in split:
        draws = jax.random.uniform(jax.random.fold_in(jax.random.fold_in(stream_key, 6), position), (parts,), jnp.float32, smallest / len(split), high / len(split))
        loudness = loudness * jnp.repeat(jnp.exp(draws), dims[position] // parts).reshape((-1,) + (1,) * (len(dims) - 1 - position))
    return loudness


def noise(key, extent, scale, reach, cuts=(), kind=jnp.bfloat16):
    result = scale * jax.random.normal(key, extent, jnp.float32)
    if cuts:
        result = result * block_levels(key, extent, cuts, -0.22, 0.18)
    return jnp.clip(result, -reach, reach).astype(kind)


def setup_inputs(seed: int = 0) -> dict:
    streams_of = jax.random.split(jax.random.key(seed), 3)
    source = noise(streams_of[0], (NT, NZ, NYX, DOF, RHS), 1.0, 6.0, ((0, 16), (1, 16)))
    link_blocks = noise(streams_of[1], (NT, NZ, NYX, DIRS, DOF, DOF), (DIRS * DOF) ** -0.5, 0.21875, ((0, 16), (1, 16)))
    return {"source": source, "link_blocks": link_blocks}


def apply_whole(vectors, link_blocks):
    def one_slice(t_index):
        here = lax.dynamic_index_in_dim(vectors, t_index, 0, keepdims=False)
        after = lax.dynamic_index_in_dim(vectors, (t_index + 1) % NT, 0, keepdims=False)
        before = lax.dynamic_index_in_dim(vectors, (t_index + NT - 1) % NT, 0, keepdims=False)
        links_here = lax.dynamic_index_in_dim(link_blocks, t_index, 0, keepdims=False)
        planes = here.reshape(NZ, NY, NX, DOF, RHS)
        neighbours = [
            here,
            jnp.roll(planes, -1, axis=2).reshape(NZ, NYX, DOF, RHS),
            jnp.roll(planes, 1, axis=2).reshape(NZ, NYX, DOF, RHS),
            jnp.roll(planes, -1, axis=1).reshape(NZ, NYX, DOF, RHS),
            jnp.roll(planes, 1, axis=1).reshape(NZ, NYX, DOF, RHS),
            jnp.roll(here, -1, axis=0),
            jnp.roll(here, 1, axis=0),
            after,
            before,
        ]
        summed = jnp.zeros((NZ, NYX, DOF, RHS), jnp.float32)
        for direction in range(DIRS):
            link_block = links_here[:, :, direction].astype(jnp.float32)
            neighbour = neighbours[direction].astype(jnp.float32)
            summed = summed + jnp.einsum("zsab,zsbr->zsar", link_block, neighbour)
        return summed

    return lax.map(one_slice, jnp.arange(NT, dtype=jnp.int32))


def reference(source, link_blocks):
    vectors = source
    for apply_step in range(APPLIES):
        summed = apply_whole(vectors, link_blocks)
        if apply_step < APPLIES - 1:
            vectors = summed.astype(jnp.bfloat16)
        else:
            vectors = summed
    return vectors
```

```python
import functools

import jax
import jax.numpy as jnp
from jax import lax
from jax.experimental import pallas as pl
from jax.experimental.pallas import tpu as pltpu
from jax.sharding import PartitionSpec as P

DOF = 96
DIRS = 9
RHS = 128
NX = 8
NY = 2
NYX = NX * NY
APPLIES = 4
CHUNK = 2
CHUNKS = NYX // CHUNK

FACES = 4


def kernel(src, links_hbm, out, links, vecs, faces, summed, load_sem, send_sem, recv_sem, out_sem):
    t, z = lax.axis_index("ta"), lax.axis_index("gz")
    nt, nz = lax.axis_size("ta"), lax.axis_size("gz")
    t_up, t_down = lax.rem(t + 1, nt), lax.rem(t + nt - 1, nt)
    z_up, z_down = lax.rem(z + 1, nz), lax.rem(z + nz - 1, nz)
    targets = [(t, z_down), (t, z_up), (t_down, z), (t_up, z)]

    load_links = pltpu.make_async_copy(links_hbm, links, load_sem.at[0])
    load_source = pltpu.make_async_copy(src, vecs.at[0], load_sem.at[1])
    load_source.start()
    load_links.start()

    barrier = pltpu.get_barrier_semaphore()
    for target in targets:
        pl.semaphore_signal(barrier, inc=1, device_id=target, device_id_type=pl.DeviceIdType.MESH)
    pl.semaphore_wait(barrier, FACES)

    def push(block, k, c, face):
        return pltpu.make_async_remote_copy(
            src_ref=block,
            dst_ref=faces.at[k, face, pl.ds(c * CHUNK, CHUNK)],
            send_sem=send_sem.at[k, face],
            recv_sem=recv_sem.at[k, face, c],
            device_id=targets[face],
            device_id_type=pl.DeviceIdType.MESH,
        )

    for c in range(CHUNKS):
        for face in range(FACES):
            push(src.at[pl.ds(c * CHUNK, CHUNK)], 0, c, face).start()
    load_source.wait()
    load_links.wait()

    def applied(k, s):
        row, x = s // NX, lax.rem(s, NX)
        here = [
            s,
            row * NX + lax.rem(x + 1, NX),
            row * NX + lax.rem(x + NX - 1, NX),
            lax.rem(s + NX, NYX),
            lax.rem(s + NX, NYX),
        ]
        total = jnp.zeros((DOF, RHS), jnp.float32)
        for d, at in enumerate(here):
            total += jnp.dot(links[s, d], vecs[k, at], preferred_element_type=jnp.float32)
        for face in range(FACES):
            total += jnp.dot(links[s, 5 + face], faces[k, face, s], preferred_element_type=jnp.float32)
        return total

    def arrived(k, c):
        for face in range(FACES):
            push(vecs.at[k, pl.ds(c * CHUNK, CHUNK)], k, c, face).wait_recv()

    def sent(k):
        for face in range(FACES):
            pltpu.make_async_remote_copy(
                src_ref=vecs.at[k],
                dst_ref=faces.at[k, face],
                send_sem=send_sem.at[k, face],
                recv_sem=recv_sem.at[k, face, 0],
                device_id=targets[face],
                device_id_type=pl.DeviceIdType.MESH,
            ).wait_send()

    @pl.loop(0, (APPLIES - 1) * CHUNKS)
    def _(step):
        k, c = step // CHUNKS, lax.rem(step, CHUNKS)
        arrived(k, c)
        for i in range(CHUNK):
            s = c * CHUNK + i
            vecs[k + 1, s] = applied(k, s).astype(jnp.bfloat16)
        for face in range(FACES):
            push(vecs.at[k + 1, pl.ds(c * CHUNK, CHUNK)], k + 1, c, face).start()

    def store(c):
        part = pl.ds(c * CHUNK, CHUNK)
        return pltpu.make_async_copy(summed.at[part], out.at[part], out_sem.at[c])

    @pl.loop(0, CHUNKS)
    def _(c):
        arrived(APPLIES - 1, c)
        for i in range(CHUNK):
            s = c * CHUNK + i
            summed[s] = applied(APPLIES - 1, s)
        store(c).start()

    for k in range(APPLIES):
        sent(k)
    for c in range(CHUNKS):
        store(c).wait()


def shards(source, link_blocks):
    src = source.reshape(NYX, DOF, RHS)
    links = link_blocks.reshape(NYX, DIRS, DOF, DOF)
    total = pl.pallas_call(
        kernel,
        out_shape=jax.ShapeDtypeStruct((NYX, DOF, RHS), jnp.float32),
        in_specs=[pl.BlockSpec(memory_space=pl.ANY)] * 2,
        out_specs=pl.BlockSpec(memory_space=pl.ANY),
        scratch_shapes=[
            pltpu.VMEM((NYX, DIRS, DOF, DOF), jnp.bfloat16),
            pltpu.VMEM((APPLIES, NYX, DOF, RHS), jnp.bfloat16),
            pltpu.VMEM((APPLIES, FACES, NYX, DOF, RHS), jnp.bfloat16),
            pltpu.VMEM((NYX, DOF, RHS), jnp.float32),
            pltpu.SemaphoreType.DMA((2,)),
            pltpu.SemaphoreType.DMA((APPLIES, FACES)),
            pltpu.SemaphoreType.DMA((APPLIES, FACES, CHUNKS)),
            pltpu.SemaphoreType.DMA((CHUNKS,)),
        ],
        compiler_params=pltpu.CompilerParams(
            collective_id=0, has_side_effects=True, vmem_limit_bytes=56 * 2**20
        ),
        cost_estimate=pl.CostEstimate(
            flops=2 * APPLIES * NYX * DIRS * DOF * DOF * RHS, bytes_accessed=6 * 2**20, transcendentals=0
        ),
    )(src, links)
    return total.reshape(1, 1, NYX, DOF, RHS)


def solution(mesh):
    placed = (P("ta", "gz", None, None, None), P("ta", "gz", None, None, None, None))
    return jax.shard_map(
        shards,
        mesh=mesh,
        in_specs=placed,
        out_specs=P("ta", "gz", None, None, None),
        check_vma=False,
    )
```

```python
import jax
import jax.numpy as jnp
from jax import lax
from jax.experimental import pallas as pl
from jax.experimental.pallas import tpu as pltpu
from jax.sharding import PartitionSpec as P

DOF = 96
DIRS = 9
RHS = 128
NX = 8
NY = 2
NYX = NX * NY
APPLIES = 4
CHUNK = 2
CHUNKS = NYX // CHUNK
STEPS = APPLIES * CHUNKS
DIRECT = CHUNKS
RELAY = CHUNKS
PASS = 4

FACES = 4
MESH = pl.DeviceIdType.MESH


def kernel(src, links_hbm, out, links, vecs, faces, relayed, summed, load_sem, send_sem, recv_sem, relay_sem, pass_sem, out_sem):
    t, z = lax.axis_index("ta"), lax.axis_index("gz")
    nt, nz = lax.axis_size("ta"), lax.axis_size("gz")
    half = nt // 2
    edge = lax.rem(t + 1, half) < 2
    high = t // half
    last = lax.rem(t, half) // (half - 1)
    partner = lax.rem(t + half, nt)

    z_out, z_out_face = lax.rem(z + high + (1 - high) * (nz - 1), nz), high
    z_over, z_over_face = lax.rem(z + (1 - high) + high * (nz - 1), nz), 1 - high
    t_in, t_in_face = lax.rem(t + (1 - last) + last * (nt - 1), nt), 3 - last
    t_over, t_over_face = lax.rem(t + last + (1 - last) * (nt - 1), nt), 2 + last
    t_pass = lax.rem(t_over + half, nt)

    load_links = pltpu.make_async_copy(links_hbm, links, load_sem.at[0])
    load_source = pltpu.make_async_copy(src, vecs.at[0], load_sem.at[1])
    load_source.start()
    load_links.start()

    barrier = pltpu.get_barrier_semaphore()

    def greet(target):
        pl.semaphore_signal(barrier, inc=1, device_id=target, device_id_type=MESH)

    greet((t, z_out))
    greet((t_in, z))
    greet((t, z_over))

    @pl.when(edge)
    def _():
        greet((partner, z))
        greet((partner, z_out))
        greet((t_pass, z))
        pl.semaphore_wait(barrier, 6)

    @pl.when(jnp.logical_not(edge))
    def _():
        greet((t_over, z))
        pl.semaphore_wait(barrier, 4)

    def remote(block, slot, send, recv, target):
        return pltpu.make_async_remote_copy(
            src_ref=block, dst_ref=slot, send_sem=send, recv_sem=recv, device_id=target, device_id_type=MESH
        )

    def part(c):
        return pl.ds(c * CHUNK, CHUNK)

    def push(block, k, c, face, target):
        remote(block, faces.at[k, face, part(c)], send_sem.at[k, face], recv_sem.at[k, face, c], target).start()

    def issue_relay(block, k, c):
        @pl.when(edge)
        def _():
            remote(
                block, relayed.at[k, part(c)], send_sem.at[k, z_over_face], relay_sem.at[k, c], (partner, z)
            ).start()

    def issue_direct(block, k, c):
        push(block, k, c, z_out_face, (t, z_out))

        @pl.when(jnp.logical_not(edge))
        def _():
            push(block, k, c, z_over_face, (t, z_over))
            push(block, k, c, t_over_face, (t_over, z))

        push(block, k, c, t_in_face, (t_in, z))

    def passed(k, c):
        block = relayed.at[k, part(c)]
        on_z = remote(
            block, faces.at[k, z_out_face, part(c)], pass_sem.at[k, 0], recv_sem.at[k, z_out_face, c], (partner, z_out)
        )
        on_t = remote(
            block, faces.at[k, t_over_face, part(c)], pass_sem.at[k, 1], recv_sem.at[k, t_over_face, c], (t_pass, z)
        )
        return on_z, on_t

    def issue_pass(k, c):
        @pl.when(edge)
        def _():
            remote(
                vecs.at[k, part(c)], relayed.at[k, part(c)], send_sem.at[k, 0], relay_sem.at[k, c], (partner, z)
            ).wait_recv()
            on_z, on_t = passed(k, c)
            on_z.start()
            on_t.start()

    def arrived(k, c):
        for face in range(FACES):
            remote(
                vecs.at[k, part(c)], faces.at[k, face, part(c)], send_sem.at[k, face], recv_sem.at[k, face, c], (t_in, z)
            ).wait_recv()

    def applied(k, s):
        row, x = s // NX, lax.rem(s, NX)
        here = [
            s,
            row * NX + lax.rem(x + 1, NX),
            row * NX + lax.rem(x + NX - 1, NX),
            lax.rem(s + NX, NYX),
            lax.rem(s + NX, NYX),
        ]
        total = jnp.zeros((DOF, RHS), jnp.float32)
        for d, at in enumerate(here):
            total += jnp.dot(links[s, d], vecs[k, at], preferred_element_type=jnp.float32)
        for face in range(FACES):
            total += jnp.dot(links[s, 5 + face], faces[k, face, s], preferred_element_type=jnp.float32)
        return total

    def whose(step):
        return step // CHUNKS, lax.rem(step, CHUNKS)

    def direct_at(step):
        k, c = whose(step)
        issue_direct(vecs.at[k, part(c)], k, c)

    def relay_at(step):
        k, c = whose(step)
        issue_relay(vecs.at[k, part(c)], k, c)

    for c in range(RELAY):
        issue_relay(src.at[part(c)], 0, c)
        if c < PASS:
            issue_direct(src.at[part(c)], 0, c)
    for c in range(PASS):
        issue_pass(0, c)
    for c in range(PASS, DIRECT):
        issue_direct(src.at[part(c)], 0, c)
    load_source.wait()
    load_links.wait()

    @pl.loop(0, STEPS - CHUNKS)
    def _(step):
        k, c = whose(step)
        arrived(k, c)
        for i in range(CHUNK):
            s = c * CHUNK + i
            vecs[k + 1, s] = applied(k, s).astype(jnp.bfloat16)
        relay_at(step + RELAY)
        issue_pass(*whose(step + PASS))
        direct_at(step + DIRECT)

    def store(c):
        return pltpu.make_async_copy(summed.at[part(c)], out.at[part(c)], out_sem.at[c])

    @pl.loop(0, CHUNKS)
    def _(c):
        arrived(APPLIES - 1, c)

        @pl.when(c + PASS < CHUNKS)
        def _():
            issue_pass(APPLIES - 1, c + PASS)

        for i in range(CHUNK):
            s = c * CHUNK + i
            summed[s] = applied(APPLIES - 1, s)
        store(c).start()

    def sent(k, sem):
        remote(vecs.at[k], faces.at[k, 0], sem, recv_sem.at[k, 0, 0], (t_in, z)).wait_send()

    for k in range(APPLIES):
        sent(k, send_sem.at[k, z_out_face])
        sent(k, send_sem.at[k, z_over_face])
        sent(k, send_sem.at[k, t_in_face])

        @pl.when(edge)
        def _():
            sent(k, pass_sem.at[k, 0])
            sent(k, pass_sem.at[k, 1])

        @pl.when(jnp.logical_not(edge))
        def _():
            sent(k, send_sem.at[k, t_over_face])

    for c in range(CHUNKS):
        store(c).wait()


def shards(source, link_blocks):
    src = source.reshape(NYX, DOF, RHS)
    links = link_blocks.reshape(NYX, DIRS, DOF, DOF)
    total = pl.pallas_call(
        kernel,
        out_shape=jax.ShapeDtypeStruct((NYX, DOF, RHS), jnp.float32),
        in_specs=[pl.BlockSpec(memory_space=pl.ANY)] * 2,
        out_specs=pl.BlockSpec(memory_space=pl.ANY),
        scratch_shapes=[
            pltpu.VMEM((NYX, DIRS, DOF, DOF), jnp.bfloat16),
            pltpu.VMEM((APPLIES, NYX, DOF, RHS), jnp.bfloat16),
            pltpu.VMEM((APPLIES, FACES, NYX, DOF, RHS), jnp.bfloat16),
            pltpu.VMEM((APPLIES, NYX, DOF, RHS), jnp.bfloat16),
            pltpu.VMEM((NYX, DOF, RHS), jnp.float32),
            pltpu.SemaphoreType.DMA((2,)),
            pltpu.SemaphoreType.DMA((APPLIES, FACES)),
            pltpu.SemaphoreType.DMA((APPLIES, FACES, CHUNKS)),
            pltpu.SemaphoreType.DMA((APPLIES, CHUNKS)),
            pltpu.SemaphoreType.DMA((APPLIES, 2)),
            pltpu.SemaphoreType.DMA((CHUNKS,)),
        ],
        compiler_params=pltpu.CompilerParams(
            collective_id=0, has_side_effects=True, vmem_limit_bytes=56 * 2**20
        ),
        cost_estimate=pl.CostEstimate(
            flops=2 * APPLIES * NYX * DIRS * DOF * DOF * RHS, bytes_accessed=6 * 2**20, transcendentals=0
        ),
    )(src, links)
    return total.reshape(1, 1, NYX, DOF, RHS)


def solution(mesh):
    placed = (P("ta", "gz", None, None, None), P("ta", "gz", None, None, None, None))
    return jax.shard_map(
        shards,
        mesh=mesh,
        in_specs=placed,
        out_specs=P("ta", "gz", None, None, None),
        check_vma=False,
    )
```

```python
import jax
import jax.numpy as jnp
from jax import lax
from jax.experimental import pallas as pl
from jax.experimental.pallas import tpu as pltpu
from jax.sharding import PartitionSpec as P

DOF = 96
DIRS = 9
RHS = 128
NX = 8
NY = 2
NYX = NX * NY
APPLIES = 4
CHUNK = 2
CHUNKS = NYX // CHUNK
STEPS = APPLIES * CHUNKS
DIRECT = CHUNKS
DIRECT_EDGE = 5
RELAY = CHUNKS
PASS = 5

FACES = 4
MESH = pl.DeviceIdType.MESH


def kernel(src, links_hbm, out, links, vecs, faces, relayed, summed, load_sem, send_sem, recv_sem, relay_sem, pass_sem, out_sem):
    t, z = lax.axis_index("ta"), lax.axis_index("gz")
    nt, nz = lax.axis_size("ta"), lax.axis_size("gz")
    half = nt // 2
    edge = lax.rem(t + 1, half) < 2
    high = t // half
    last = lax.rem(t, half) // (half - 1)
    partner = lax.rem(t + half, nt)

    z_out, z_out_face = lax.rem(z + high + (1 - high) * (nz - 1), nz), high
    z_over, z_over_face = lax.rem(z + (1 - high) + high * (nz - 1), nz), 1 - high
    t_in, t_in_face = lax.rem(t + (1 - last) + last * (nt - 1), nt), 3 - last
    t_over, t_over_face = lax.rem(t + last + (1 - last) * (nt - 1), nt), 2 + last
    t_pass = lax.rem(t_over + half, nt)

    load_links = pltpu.make_async_copy(links_hbm, links, load_sem.at[0])
    load_source = pltpu.make_async_copy(src, vecs.at[0], load_sem.at[1])
    load_source.start()
    load_links.start()

    barrier = pltpu.get_barrier_semaphore()

    def greet(target):
        pl.semaphore_signal(barrier, inc=1, device_id=target, device_id_type=MESH)

    greet((t, z_out))
    greet((t_in, z))
    greet((t, z_over))

    @pl.when(edge)
    def _():
        greet((partner, z))
        greet((partner, z_out))
        greet((t_pass, z))
        pl.semaphore_wait(barrier, 6)

    @pl.when(jnp.logical_not(edge))
    def _():
        greet((t_over, z))
        pl.semaphore_wait(barrier, 4)

    def remote(block, slot, send, recv, target):
        return pltpu.make_async_remote_copy(
            src_ref=block, dst_ref=slot, send_sem=send, recv_sem=recv, device_id=target, device_id_type=MESH
        )

    def part(c):
        return pl.ds(c * CHUNK, CHUNK)

    def push(block, k, c, face, target):
        remote(block, faces.at[k, face, part(c)], send_sem.at[k, face], recv_sem.at[k, face, c], target).start()

    def issue_relay(block, k, c):
        @pl.when(edge)
        def _():
            remote(
                block, relayed.at[k, part(c)], send_sem.at[k, z_over_face], relay_sem.at[k, c], (partner, z)
            ).start()

    def issue_edge(block, k, c):
        @pl.when(edge)
        def _():
            push(block, k, c, z_out_face, (t, z_out))
            push(block, k, c, t_in_face, (t_in, z))

    def issue_inner(block, k, c):
        @pl.when(jnp.logical_not(edge))
        def _():
            push(block, k, c, z_out_face, (t, z_out))
            push(block, k, c, z_over_face, (t, z_over))
            push(block, k, c, t_over_face, (t_over, z))
            push(block, k, c, t_in_face, (t_in, z))

    def passed(k, c):
        block = relayed.at[k, part(c)]
        on_z = remote(
            block, faces.at[k, z_out_face, part(c)], pass_sem.at[k, 0], recv_sem.at[k, z_out_face, c], (partner, z_out)
        )
        on_t = remote(
            block, faces.at[k, t_over_face, part(c)], pass_sem.at[k, 1], recv_sem.at[k, t_over_face, c], (t_pass, z)
        )
        return on_z, on_t

    def issue_pass(k, c):
        @pl.when(edge)
        def _():
            remote(
                vecs.at[k, part(c)], relayed.at[k, part(c)], send_sem.at[k, 0], relay_sem.at[k, c], (partner, z)
            ).wait_recv()
            on_z, on_t = passed(k, c)
            on_z.start()
            on_t.start()

    def arrived(k, c):
        for face in range(FACES):
            remote(
                vecs.at[k, part(c)], faces.at[k, face, part(c)], send_sem.at[k, face], recv_sem.at[k, face, c], (t_in, z)
            ).wait_recv()

    def applied(k, s):
        row, x = s // NX, lax.rem(s, NX)
        here = [
            s,
            row * NX + lax.rem(x + 1, NX),
            row * NX + lax.rem(x + NX - 1, NX),
            lax.rem(s + NX, NYX),
            lax.rem(s + NX, NYX),
        ]
        total = jnp.zeros((DOF, RHS), jnp.float32)
        for d, at in enumerate(here):
            total += jnp.dot(links[s, d], vecs[k, at], preferred_element_type=jnp.float32)
        for face in range(FACES):
            total += jnp.dot(links[s, 5 + face], faces[k, face, s], preferred_element_type=jnp.float32)
        return total

    def whose(step):
        return step // CHUNKS, lax.rem(step, CHUNKS)

    def send(issue, step):
        k, c = whose(step)
        issue(vecs.at[k, part(c)], k, c)

    for c in range(CHUNKS):
        issue_relay(src.at[part(c)], 0, c)
        issue_inner(src.at[part(c)], 0, c)
        if c < DIRECT_EDGE:
            issue_edge(src.at[part(c)], 0, c)
        if c >= CHUNKS - PASS:
            issue_pass(0, c - (CHUNKS - PASS))
    load_source.wait()
    load_links.wait()

    @pl.loop(0, STEPS - CHUNKS)
    def _(step):
        k, c = whose(step)
        arrived(k, c)
        send(issue_edge, step + DIRECT_EDGE)
        for i in range(CHUNK):
            s = c * CHUNK + i
            vecs[k + 1, s] = applied(k, s).astype(jnp.bfloat16)
        send(issue_relay, step + RELAY)
        send(issue_inner, step + DIRECT)
        issue_pass(*whose(step + PASS))

    def store(c):
        return pltpu.make_async_copy(summed.at[part(c)], out.at[part(c)], out_sem.at[c])

    @pl.loop(0, CHUNKS)
    def _(c):
        arrived(APPLIES - 1, c)

        @pl.when(c + DIRECT_EDGE < CHUNKS)
        def _():
            send(issue_edge, STEPS - CHUNKS + c + DIRECT_EDGE)

        @pl.when(c + PASS < CHUNKS)
        def _():
            issue_pass(APPLIES - 1, c + PASS)

        for i in range(CHUNK):
            s = c * CHUNK + i
            summed[s] = applied(APPLIES - 1, s)
        store(c).start()

    def sent(k, sem):
        remote(vecs.at[k], faces.at[k, 0], sem, recv_sem.at[k, 0, 0], (t_in, z)).wait_send()

    for k in range(APPLIES):
        sent(k, send_sem.at[k, z_out_face])
        sent(k, send_sem.at[k, z_over_face])
        sent(k, send_sem.at[k, t_in_face])

        @pl.when(edge)
        def _():
            sent(k, pass_sem.at[k, 0])
            sent(k, pass_sem.at[k, 1])

        @pl.when(jnp.logical_not(edge))
        def _():
            sent(k, send_sem.at[k, t_over_face])

    for c in range(CHUNKS):
        store(c).wait()


def shards(source, link_blocks):
    src = pltpu.with_memory_space_constraint(source.reshape(NYX, DOF, RHS), pltpu.HBM)
    links = pltpu.with_memory_space_constraint(link_blocks.reshape(NYX, DIRS, DOF, DOF), pltpu.HBM)
    total = pl.pallas_call(
        kernel,
        out_shape=jax.ShapeDtypeStruct((NYX, DOF, RHS), jnp.float32),
        in_specs=[pl.BlockSpec(memory_space=pl.ANY)] * 2,
        out_specs=pl.BlockSpec(memory_space=pl.ANY),
        scratch_shapes=[
            pltpu.VMEM((NYX, DIRS, DOF, DOF), jnp.bfloat16),
            pltpu.VMEM((APPLIES, NYX, DOF, RHS), jnp.bfloat16),
            pltpu.VMEM((APPLIES, FACES, NYX, DOF, RHS), jnp.bfloat16),
            pltpu.VMEM((APPLIES, NYX, DOF, RHS), jnp.bfloat16),
            pltpu.VMEM((NYX, DOF, RHS), jnp.float32),
            pltpu.SemaphoreType.DMA((2,)),
            pltpu.SemaphoreType.DMA((APPLIES, FACES)),
            pltpu.SemaphoreType.DMA((APPLIES, FACES, CHUNKS)),
            pltpu.SemaphoreType.DMA((APPLIES, CHUNKS)),
            pltpu.SemaphoreType.DMA((APPLIES, 2)),
            pltpu.SemaphoreType.DMA((CHUNKS,)),
        ],
        compiler_params=pltpu.CompilerParams(
            collective_id=0, has_side_effects=True, vmem_limit_bytes=40 * 2**20
        ),
        cost_estimate=pl.CostEstimate(
            flops=2 * APPLIES * NYX * DIRS * DOF * DOF * RHS, bytes_accessed=6 * 2**20, transcendentals=0
        ),
    )(src, links)
    return total.reshape(1, 1, NYX, DOF, RHS)


def solution(mesh):
    placed = (P("ta", "gz", None, None, None), P("ta", "gz", None, None, None, None))
    return jax.shard_map(
        shards,
        mesh=mesh,
        in_specs=placed,
        out_specs=P("ta", "gz", None, None, None),
        check_vma=False,
    )
```

```python
import jax
import jax.numpy as jnp
from jax import lax
from jax.experimental import pallas as pl
from jax.experimental.pallas import tpu as pltpu
from jax.sharding import PartitionSpec as P

DOF = 96
DIRS = 9
RHS = 128
NX = 8
NY = 2
NYX = NX * NY
APPLIES = 4
CHUNK = 1
CHUNKS = NYX // CHUNK
STEPS = APPLIES * CHUNKS
DIRECT = 13
DIRECT_EDGE = 10
RELAY = CHUNKS
PASS = 5
FIRST = 3

FACES = 4
MESH = pl.DeviceIdType.MESH


def kernel(src, links_hbm, out, links, vecs, faces, relayed, summed, load_sem, send_sem, recv_sem, relay_sem, pass_sem, out_sem):
    t, z = lax.axis_index("ta"), lax.axis_index("gz")
    nt, nz = lax.axis_size("ta"), lax.axis_size("gz")
    half = nt // 2
    edge = lax.rem(t + 1, half) < 2
    high = t // half
    last = lax.rem(t, half) // (half - 1)
    partner = lax.rem(t + half, nt)

    z_out, z_out_face = lax.rem(z + high + (1 - high) * (nz - 1), nz), high
    z_over, z_over_face = lax.rem(z + (1 - high) + high * (nz - 1), nz), 1 - high
    t_in, t_in_face = lax.rem(t + (1 - last) + last * (nt - 1), nt), 3 - last
    t_over, t_over_face = lax.rem(t + last + (1 - last) * (nt - 1), nt), 2 + last
    t_pass = lax.rem(t_over + half, nt)

    load_links = pltpu.make_async_copy(links_hbm, links, load_sem.at[0])
    load_source = pltpu.make_async_copy(src, vecs.at[0], load_sem.at[1])
    load_source.start()
    load_links.start()

    barrier = pltpu.get_barrier_semaphore()

    def greet(target):
        pl.semaphore_signal(barrier, inc=1, device_id=target, device_id_type=MESH)

    greet((t, z_out))
    greet((t_in, z))
    greet((t, z_over))

    @pl.when(edge)
    def _():
        greet((partner, z))
        greet((partner, z_out))
        greet((t_pass, z))
        pl.semaphore_wait(barrier, 6)

    @pl.when(jnp.logical_not(edge))
    def _():
        greet((t_over, z))
        pl.semaphore_wait(barrier, 4)

    def remote(block, slot, send, recv, target):
        return pltpu.make_async_remote_copy(
            src_ref=block, dst_ref=slot, send_sem=send, recv_sem=recv, device_id=target, device_id_type=MESH
        )

    def part(c):
        return pl.ds(c * CHUNK, CHUNK)

    def push(block, k, c, face, target):
        remote(block, faces.at[k, face, part(c)], send_sem.at[k, face], recv_sem.at[k, face, c], target).start()

    def issue_relay(block, k, c):
        @pl.when(edge)
        def _():
            remote(
                block, relayed.at[k, part(c)], send_sem.at[k, z_over_face], relay_sem.at[k, c], (partner, z)
            ).start()

    def issue_edge(block, k, c):
        @pl.when(edge)
        def _():
            push(block, k, c, z_out_face, (t, z_out))
            push(block, k, c, t_in_face, (t_in, z))

    def issue_inner(block, k, c):
        @pl.when(jnp.logical_not(edge))
        def _():
            push(block, k, c, z_out_face, (t, z_out))
            push(block, k, c, z_over_face, (t, z_over))
            push(block, k, c, t_over_face, (t_over, z))
            push(block, k, c, t_in_face, (t_in, z))

    def passed(k, c):
        block = relayed.at[k, part(c)]
        on_z = remote(
            block, faces.at[k, z_out_face, part(c)], pass_sem.at[k, 0], recv_sem.at[k, z_out_face, c], (partner, z_out)
        )
        on_t = remote(
            block, faces.at[k, t_over_face, part(c)], pass_sem.at[k, 1], recv_sem.at[k, t_over_face, c], (t_pass, z)
        )
        return on_z, on_t

    def issue_pass(k, c):
        @pl.when(edge)
        def _():
            remote(
                vecs.at[k, part(c)], relayed.at[k, part(c)], send_sem.at[k, 0], relay_sem.at[k, c], (partner, z)
            ).wait_recv()
            on_z, on_t = passed(k, c)
            on_z.start()
            on_t.start()

    def arrived(k, c):
        for face in range(FACES):
            remote(
                vecs.at[k, part(c)], faces.at[k, face, part(c)], send_sem.at[k, face], recv_sem.at[k, face, c], (t_in, z)
            ).wait_recv()

    def applied(k, s):
        row, x = s // NX, lax.rem(s, NX)
        here = [
            s,
            row * NX + lax.rem(x + 1, NX),
            row * NX + lax.rem(x + NX - 1, NX),
            lax.rem(s + NX, NYX),
            lax.rem(s + NX, NYX),
        ]
        total = jnp.zeros((DOF, RHS), jnp.float32)
        for d, at in enumerate(here):
            total += jnp.dot(links[s, d], vecs[k, at], preferred_element_type=jnp.float32)
        for face in range(FACES):
            total += jnp.dot(links[s, 5 + face], faces[k, face, s], preferred_element_type=jnp.float32)
        return total

    def whose(step):
        return step // CHUNKS, lax.rem(step, CHUNKS)

    def send(issue, step):
        k, c = whose(step)
        issue(vecs.at[k, part(c)], k, c)

    for c in range(CHUNKS):
        issue_relay(src.at[part(c)], 0, c)
        if c < DIRECT:
            issue_inner(src.at[part(c)], 0, c)
        if c < DIRECT_EDGE:
            issue_edge(src.at[part(c)], 0, c)
        if FIRST <= c < FIRST + PASS:
            issue_pass(0, c - FIRST)
    load_source.wait()
    load_links.wait()

    @pl.loop(0, STEPS - CHUNKS)
    def _(step):
        k, c = whose(step)
        arrived(k, c)
        send(issue_edge, step + DIRECT_EDGE)
        send(issue_inner, step + DIRECT)
        for i in range(CHUNK):
            s = c * CHUNK + i
            vecs[k + 1, s] = applied(k, s).astype(jnp.bfloat16)
        send(issue_relay, step + RELAY)
        issue_pass(*whose(step + PASS))

    def store(c):
        return pltpu.make_async_copy(summed.at[part(c)], out.at[part(c)], out_sem.at[c])

    @pl.loop(0, CHUNKS)
    def _(c):
        arrived(APPLIES - 1, c)

        @pl.when(c + DIRECT_EDGE < CHUNKS)
        def _():
            send(issue_edge, STEPS - CHUNKS + c + DIRECT_EDGE)

        @pl.when(c + DIRECT < CHUNKS)
        def _():
            send(issue_inner, STEPS - CHUNKS + c + DIRECT)

        @pl.when(c + PASS < CHUNKS)
        def _():
            issue_pass(APPLIES - 1, c + PASS)

        for i in range(CHUNK):
            s = c * CHUNK + i
            summed[s] = applied(APPLIES - 1, s)
        store(c).start()

    def sent(k, sem):
        remote(vecs.at[k], faces.at[k, 0], sem, recv_sem.at[k, 0, 0], (t_in, z)).wait_send()

    for k in range(APPLIES):
        sent(k, send_sem.at[k, z_out_face])
        sent(k, send_sem.at[k, z_over_face])
        sent(k, send_sem.at[k, t_in_face])

        @pl.when(edge)
        def _():
            sent(k, pass_sem.at[k, 0])
            sent(k, pass_sem.at[k, 1])

        @pl.when(jnp.logical_not(edge))
        def _():
            sent(k, send_sem.at[k, t_over_face])

    for c in range(CHUNKS):
        store(c).wait()


def shards(source, link_blocks):
    src = pltpu.with_memory_space_constraint(source.reshape(NYX, DOF, RHS), pltpu.HBM)
    links = pltpu.with_memory_space_constraint(link_blocks.reshape(NYX, DIRS, DOF, DOF), pltpu.HBM)
    total = pl.pallas_call(
        kernel,
        out_shape=jax.ShapeDtypeStruct((NYX, DOF, RHS), jnp.float32),
        in_specs=[pl.BlockSpec(memory_space=pl.ANY)] * 2,
        out_specs=pl.BlockSpec(memory_space=pl.ANY),
        scratch_shapes=[
            pltpu.VMEM((NYX, DIRS, DOF, DOF), jnp.bfloat16),
            pltpu.VMEM((APPLIES, NYX, DOF, RHS), jnp.bfloat16),
            pltpu.VMEM((APPLIES, FACES, NYX, DOF, RHS), jnp.bfloat16),
            pltpu.VMEM((APPLIES, NYX, DOF, RHS), jnp.bfloat16),
            pltpu.VMEM((NYX, DOF, RHS), jnp.float32),
            pltpu.SemaphoreType.DMA((2,)),
            pltpu.SemaphoreType.DMA((APPLIES, FACES)),
            pltpu.SemaphoreType.DMA((APPLIES, FACES, CHUNKS)),
            pltpu.SemaphoreType.DMA((APPLIES, CHUNKS)),
            pltpu.SemaphoreType.DMA((APPLIES, 2)),
            pltpu.SemaphoreType.DMA((CHUNKS,)),
        ],
        compiler_params=pltpu.CompilerParams(
            collective_id=0, has_side_effects=True, vmem_limit_bytes=40 * 2**20
        ),
        cost_estimate=pl.CostEstimate(
            flops=2 * APPLIES * NYX * DIRS * DOF * DOF * RHS, bytes_accessed=6 * 2**20, transcendentals=0
        ),
    )(src, links)
    return total.reshape(1, 1, NYX, DOF, RHS)


def solution(mesh):
    placed = (P("ta", "gz", None, None, None), P("ta", "gz", None, None, None, None))
    return jax.shard_map(
        shards,
        mesh=mesh,
        in_specs=placed,
        out_specs=P("ta", "gz", None, None, None),
        check_vma=False,
    )
```

```python
import jax
import jax.numpy as jnp
from jax import lax
from jax.experimental import pallas as pl
from jax.experimental.pallas import tpu as pltpu
from jax.sharding import PartitionSpec as P

DOF = 96
DIRS = 9
RHS = 128
NX = 8
NY = 2
NYX = NX * NY
APPLIES = 4
CHUNK = 2
CHUNKS = NYX // CHUNK
STEPS = APPLIES * CHUNKS
DIRECT = CHUNKS
DIRECT_EDGE = 5
RELAY = CHUNKS
PASS = 5
STRAIGHT = 1
RELAYED = STEPS - STRAIGHT

FACES = 4
MESH = pl.DeviceIdType.MESH


def kernel(src, links_hbm, out, links, vecs, faces, relayed, summed, load_sem, send_sem, recv_sem, relay_sem, pass_sem, out_sem):
    t, z = lax.axis_index("ta"), lax.axis_index("gz")
    nt, nz = lax.axis_size("ta"), lax.axis_size("gz")
    half = nt // 2
    edge = lax.rem(t + 1, half) < 2
    high = t // half
    last = lax.rem(t, half) // (half - 1)
    partner = lax.rem(t + half, nt)

    z_out, z_out_face = lax.rem(z + high + (1 - high) * (nz - 1), nz), high
    z_over, z_over_face = lax.rem(z + (1 - high) + high * (nz - 1), nz), 1 - high
    t_in, t_in_face = lax.rem(t + (1 - last) + last * (nt - 1), nt), 3 - last
    t_over, t_over_face = lax.rem(t + last + (1 - last) * (nt - 1), nt), 2 + last
    t_pass = lax.rem(t_over + half, nt)

    load_links = pltpu.make_async_copy(links_hbm, links, load_sem.at[0])
    load_source = pltpu.make_async_copy(src, vecs.at[0], load_sem.at[1])
    load_source.start()
    load_links.start()

    barrier = pltpu.get_barrier_semaphore()

    def greet(target):
        pl.semaphore_signal(barrier, inc=1, device_id=target, device_id_type=MESH)

    greet((t, z_out))
    greet((t_in, z))
    greet((t, z_over))
    greet((t_over, z))

    @pl.when(edge)
    def _():
        greet((partner, z))
        greet((partner, z_out))
        greet((t_pass, z))
        pl.semaphore_wait(barrier, 7)

    @pl.when(jnp.logical_not(edge))
    def _():
        pl.semaphore_wait(barrier, 4)

    def remote(block, slot, send, recv, target):
        return pltpu.make_async_remote_copy(
            src_ref=block, dst_ref=slot, send_sem=send, recv_sem=recv, device_id=target, device_id_type=MESH
        )

    def part(c):
        return pl.ds(c * CHUNK, CHUNK)

    def push(block, k, c, face, target):
        remote(block, faces.at[k, face, part(c)], send_sem.at[k, face], recv_sem.at[k, face, c], target).start()

    def issue_relay(block, k, c):
        @pl.when(jnp.logical_and(edge, k * CHUNKS + c < RELAYED))
        def _():
            remote(
                block, relayed.at[k, part(c)], send_sem.at[k, z_over_face], relay_sem.at[k, c], (partner, z)
            ).start()

    def issue_edge(block, k, c):
        @pl.when(edge)
        def _():
            push(block, k, c, z_out_face, (t, z_out))
            push(block, k, c, t_in_face, (t_in, z))

        @pl.when(jnp.logical_and(edge, k * CHUNKS + c >= RELAYED))
        def _():
            push(block, k, c, z_over_face, (t, z_over))
            push(block, k, c, t_over_face, (t_over, z))

    def issue_inner(block, k, c):
        @pl.when(jnp.logical_not(edge))
        def _():
            push(block, k, c, z_out_face, (t, z_out))
            push(block, k, c, z_over_face, (t, z_over))
            push(block, k, c, t_over_face, (t_over, z))
            push(block, k, c, t_in_face, (t_in, z))

    def passed(k, c):
        block = relayed.at[k, part(c)]
        on_z = remote(
            block, faces.at[k, z_out_face, part(c)], pass_sem.at[k, 0], recv_sem.at[k, z_out_face, c], (partner, z_out)
        )
        on_t = remote(
            block, faces.at[k, t_over_face, part(c)], pass_sem.at[k, 1], recv_sem.at[k, t_over_face, c], (t_pass, z)
        )
        return on_z, on_t

    def issue_pass(k, c):
        @pl.when(jnp.logical_and(edge, k * CHUNKS + c < RELAYED))
        def _():
            remote(
                vecs.at[k, part(c)], relayed.at[k, part(c)], send_sem.at[k, 0], relay_sem.at[k, c], (partner, z)
            ).wait_recv()
            on_z, on_t = passed(k, c)
            on_z.start()
            on_t.start()

    def arrived(k, c):
        for face in range(FACES):
            remote(
                vecs.at[k, part(c)], faces.at[k, face, part(c)], send_sem.at[k, face], recv_sem.at[k, face, c], (t_in, z)
            ).wait_recv()

    def at_home(k, s):
        row, x = s // NX, lax.rem(s, NX)
        here = [
            s,
            row * NX + lax.rem(x + 1, NX),
            row * NX + lax.rem(x + NX - 1, NX),
            lax.rem(s + NX, NYX),
            lax.rem(s + NX, NYX),
        ]
        total = jnp.zeros((DOF, RHS), jnp.float32)
        for d, at in enumerate(here):
            total += jnp.dot(links[s, d], vecs[k, at], preferred_element_type=jnp.float32)
        return total

    def applied(k, c, store_site):
        sites = [c * CHUNK + i for i in range(CHUNK)]
        totals = [at_home(k, s) for s in sites]
        arrived(k, c)
        for s, total in zip(sites, totals):
            for face in range(FACES):
                total += jnp.dot(links[s, 5 + face], faces[k, face, s], preferred_element_type=jnp.float32)
            store_site(s, total)

    def whose(step):
        return step // CHUNKS, lax.rem(step, CHUNKS)

    def send(issue, step):
        k, c = whose(step)
        issue(vecs.at[k, part(c)], k, c)

    for c in range(CHUNKS):
        issue_relay(src.at[part(c)], 0, c)
        issue_inner(src.at[part(c)], 0, c)
        if c < DIRECT_EDGE:
            issue_edge(src.at[part(c)], 0, c)
        if c >= CHUNKS - PASS:
            issue_pass(0, c - (CHUNKS - PASS))
    load_source.wait()
    load_links.wait()

    @pl.loop(0, STEPS - CHUNKS)
    def _(step):
        k, c = whose(step)

        def keep(s, total):
            vecs[k + 1, s] = total.astype(jnp.bfloat16)

        applied(k, c, keep)
        send(issue_edge, step + DIRECT_EDGE)
        send(issue_relay, step + RELAY)
        send(issue_inner, step + DIRECT)
        issue_pass(*whose(step + PASS))

    def store(c):
        return pltpu.make_async_copy(summed.at[part(c)], out.at[part(c)], out_sem.at[c])

    @pl.loop(0, CHUNKS)
    def _(c):
        def keep(s, total):
            summed[s] = total

        applied(APPLIES - 1, c, keep)

        @pl.when(c + DIRECT_EDGE < CHUNKS)
        def _():
            send(issue_edge, STEPS - CHUNKS + c + DIRECT_EDGE)

        @pl.when(c + PASS < CHUNKS)
        def _():
            issue_pass(APPLIES - 1, c + PASS)

        store(c).start()

    def sent(k, sem, chunks=CHUNKS):
        block = pl.ds(0, chunks * CHUNK)
        remote(vecs.at[k, block], faces.at[k, 0, block], sem, recv_sem.at[k, 0, 0], (t_in, z)).wait_send()

    for k in range(APPLIES):
        straight = STRAIGHT if k == APPLIES - 1 else 0
        sent(k, send_sem.at[k, z_out_face])
        sent(k, send_sem.at[k, z_over_face])
        sent(k, send_sem.at[k, t_in_face])

        @pl.when(edge)
        def _():
            sent(k, pass_sem.at[k, 0], CHUNKS - straight)
            sent(k, pass_sem.at[k, 1], CHUNKS - straight)
            if straight:
                sent(k, send_sem.at[k, t_over_face], straight)

        @pl.when(jnp.logical_not(edge))
        def _():
            sent(k, send_sem.at[k, t_over_face])

    for c in range(CHUNKS):
        store(c).wait()


def shards(source, link_blocks):
    src = pltpu.with_memory_space_constraint(source.reshape(NYX, DOF, RHS), pltpu.HBM)
    links = pltpu.with_memory_space_constraint(link_blocks.reshape(NYX, DIRS, DOF, DOF), pltpu.HBM)
    total = pl.pallas_call(
        kernel,
        out_shape=jax.ShapeDtypeStruct((NYX, DOF, RHS), jnp.float32),
        in_specs=[pl.BlockSpec(memory_space=pl.ANY)] * 2,
        out_specs=pl.BlockSpec(memory_space=pl.ANY),
        scratch_shapes=[
            pltpu.VMEM((NYX, DIRS, DOF, DOF), jnp.bfloat16),
            pltpu.VMEM((APPLIES, NYX, DOF, RHS), jnp.bfloat16),
            pltpu.VMEM((APPLIES, FACES, NYX, DOF, RHS), jnp.bfloat16),
            pltpu.VMEM((APPLIES, NYX, DOF, RHS), jnp.bfloat16),
            pltpu.VMEM((NYX, DOF, RHS), jnp.float32),
            pltpu.SemaphoreType.DMA((2,)),
            pltpu.SemaphoreType.DMA((APPLIES, FACES)),
            pltpu.SemaphoreType.DMA((APPLIES, FACES, CHUNKS)),
            pltpu.SemaphoreType.DMA((APPLIES, CHUNKS)),
            pltpu.SemaphoreType.DMA((APPLIES, 2)),
            pltpu.SemaphoreType.DMA((CHUNKS,)),
        ],
        compiler_params=pltpu.CompilerParams(
            collective_id=0, has_side_effects=True, vmem_limit_bytes=40 * 2**20
        ),
        cost_estimate=pl.CostEstimate(
            flops=2 * APPLIES * NYX * DIRS * DOF * DOF * RHS, bytes_accessed=6 * 2**20, transcendentals=0
        ),
    )(src, links)
    return total.reshape(1, 1, NYX, DOF, RHS)


def solution(mesh):
    placed = (P("ta", "gz", None, None, None), P("ta", "gz", None, None, None, None))
    return jax.shard_map(
        shards,
        mesh=mesh,
        in_specs=placed,
        out_specs=P("ta", "gz", None, None, None),
        check_vma=False,
    )
```

```python
import jax
import jax.numpy as jnp
from jax import lax
from jax.experimental import pallas as pl
from jax.experimental.pallas import tpu as pltpu
from jax.sharding import PartitionSpec as P

DOF = 96
DIRS = 9
RHS = 128
NX = 8
NY = 2
NYX = NX * NY
APPLIES = 4
CHUNK = 2
CHUNKS = NYX // CHUNK
STEPS = APPLIES * CHUNKS
DIRECT = CHUNKS
DIRECT_EDGE = 5
DIRECT_NEAR = 5
RELAY = CHUNKS
PASS = 5

FACES = 4
MESH = pl.DeviceIdType.MESH


def kernel(src, links_hbm, out, links, vecs, faces, relayed, summed, load_sem, send_sem, recv_sem, relay_sem, pass_sem, out_sem):
    t, z = lax.axis_index("ta"), lax.axis_index("gz")
    nt, nz = lax.axis_size("ta"), lax.axis_size("gz")
    half = nt // 2
    edge = lax.rem(t + 1, half) < 2
    near = jnp.logical_and(lax.rem(t + 2, half) < 4, jnp.logical_not(edge))
    inner = lax.rem(t + 2, half) >= 4
    high = t // half
    last = lax.rem(t, half) // (half - 1)
    partner = lax.rem(t + half, nt)

    z_out, z_out_face = lax.rem(z + high + (1 - high) * (nz - 1), nz), high
    z_over, z_over_face = lax.rem(z + (1 - high) + high * (nz - 1), nz), 1 - high
    t_in, t_in_face = lax.rem(t + (1 - last) + last * (nt - 1), nt), 3 - last
    t_over, t_over_face = lax.rem(t + last + (1 - last) * (nt - 1), nt), 2 + last
    t_pass = lax.rem(t_over + half, nt)

    load_links = pltpu.make_async_copy(links_hbm, links, load_sem.at[0])
    load_source = pltpu.make_async_copy(src, vecs.at[0], load_sem.at[1])
    load_source.start()
    load_links.start()

    barrier = pltpu.get_barrier_semaphore()

    def greet(target):
        pl.semaphore_signal(barrier, inc=1, device_id=target, device_id_type=MESH)

    greet((t, z_out))
    greet((t_in, z))
    greet((t, z_over))

    @pl.when(edge)
    def _():
        greet((partner, z))
        greet((partner, z_out))
        greet((t_pass, z))
        pl.semaphore_wait(barrier, 6)

    @pl.when(jnp.logical_not(edge))
    def _():
        greet((t_over, z))
        pl.semaphore_wait(barrier, 4)

    def remote(block, slot, send, recv, target):
        return pltpu.make_async_remote_copy(
            src_ref=block, dst_ref=slot, send_sem=send, recv_sem=recv, device_id=target, device_id_type=MESH
        )

    def part(c):
        return pl.ds(c * CHUNK, CHUNK)

    def push(block, k, c, face, target):
        remote(block, faces.at[k, face, part(c)], send_sem.at[k, face], recv_sem.at[k, face, c], target).start()

    def issue_relay(block, k, c):
        @pl.when(edge)
        def _():
            remote(
                block, relayed.at[k, part(c)], send_sem.at[k, z_over_face], relay_sem.at[k, c], (partner, z)
            ).start()

    def issue_edge(block, k, c):
        @pl.when(edge)
        def _():
            push(block, k, c, z_out_face, (t, z_out))
            push(block, k, c, t_in_face, (t_in, z))

    def push_all(block, k, c):
        push(block, k, c, z_out_face, (t, z_out))
        push(block, k, c, z_over_face, (t, z_over))
        push(block, k, c, t_over_face, (t_over, z))
        push(block, k, c, t_in_face, (t_in, z))

    def issue_near(block, k, c):
        @pl.when(near)
        def _():
            push_all(block, k, c)

    def issue_inner(block, k, c):
        @pl.when(inner)
        def _():
            push_all(block, k, c)

    def passed(k, c):
        block = relayed.at[k, part(c)]
        on_z = remote(
            block, faces.at[k, z_out_face, part(c)], pass_sem.at[k, 0], recv_sem.at[k, z_out_face, c], (partner, z_out)
        )
        on_t = remote(
            block, faces.at[k, t_over_face, part(c)], pass_sem.at[k, 1], recv_sem.at[k, t_over_face, c], (t_pass, z)
        )
        return on_z, on_t

    def issue_pass(k, c):
        @pl.when(edge)
        def _():
            remote(
                vecs.at[k, part(c)], relayed.at[k, part(c)], send_sem.at[k, 0], relay_sem.at[k, c], (partner, z)
            ).wait_recv()
            on_z, on_t = passed(k, c)
            on_z.start()
            on_t.start()

    def arrived(k, c):
        for face in range(FACES):
            remote(
                vecs.at[k, part(c)], faces.at[k, face, part(c)], send_sem.at[k, face], recv_sem.at[k, face, c], (t_in, z)
            ).wait_recv()

    def at_home(k, s):
        row, x = s // NX, lax.rem(s, NX)
        here = [
            s,
            row * NX + lax.rem(x + 1, NX),
            row * NX + lax.rem(x + NX - 1, NX),
            lax.rem(s + NX, NYX),
            lax.rem(s + NX, NYX),
        ]
        total = jnp.zeros((DOF, RHS), jnp.float32)
        for d, at in enumerate(here):
            total += jnp.dot(links[s, d], vecs[k, at], preferred_element_type=jnp.float32)
        return total

    def applied(k, c, store_site):
        sites = [c * CHUNK + i for i in range(CHUNK)]
        totals = [at_home(k, s) for s in sites]
        arrived(k, c)
        for s, total in zip(sites, totals):
            for face in range(FACES):
                total += jnp.dot(links[s, 5 + face], faces[k, face, s], preferred_element_type=jnp.float32)
            store_site(s, total)

    def whose(step):
        return step // CHUNKS, lax.rem(step, CHUNKS)

    def send(issue, step):
        k, c = whose(step)
        issue(vecs.at[k, part(c)], k, c)

    for c in range(CHUNKS):
        issue_relay(src.at[part(c)], 0, c)
        issue_inner(src.at[part(c)], 0, c)
        if c < DIRECT_NEAR:
            issue_near(src.at[part(c)], 0, c)
        if c < DIRECT_EDGE:
            issue_edge(src.at[part(c)], 0, c)
        if c >= CHUNKS - PASS:
            issue_pass(0, c - (CHUNKS - PASS))
    load_source.wait()
    load_links.wait()

    @pl.loop(0, STEPS - CHUNKS)
    def _(step):
        k, c = whose(step)

        def keep(s, total):
            vecs[k + 1, s] = total.astype(jnp.bfloat16)

        applied(k, c, keep)
        send(issue_edge, step + DIRECT_EDGE)
        send(issue_near, step + DIRECT_NEAR)
        send(issue_relay, step + RELAY)
        send(issue_inner, step + DIRECT)
        issue_pass(*whose(step + PASS))

    def sent(k, sem):
        remote(vecs.at[k], faces.at[k, 0], sem, recv_sem.at[k, 0, 0], (t_in, z)).wait_send()

    def sent_round(k):
        sent(k, send_sem.at[k, z_out_face])
        sent(k, send_sem.at[k, z_over_face])
        sent(k, send_sem.at[k, t_in_face])

        @pl.when(edge)
        def _():
            sent(k, pass_sem.at[k, 0])
            sent(k, pass_sem.at[k, 1])

        @pl.when(jnp.logical_not(edge))
        def _():
            sent(k, send_sem.at[k, t_over_face])

    for k in range(APPLIES - 2):
        sent_round(k)

    def store(c):
        return pltpu.make_async_copy(summed.at[part(c)], out.at[part(c)], out_sem.at[c])

    @pl.loop(0, CHUNKS)
    def _(c):
        def keep(s, total):
            summed[s] = total

        applied(APPLIES - 1, c, keep)
        store(c).start()

        @pl.when(c + DIRECT_NEAR < CHUNKS)
        def _():
            send(issue_near, STEPS - CHUNKS + c + DIRECT_NEAR)

        @pl.when(c + DIRECT_EDGE < CHUNKS)
        def _():
            send(issue_edge, STEPS - CHUNKS + c + DIRECT_EDGE)

        @pl.when(c + PASS < CHUNKS)
        def _():
            issue_pass(APPLIES - 1, c + PASS)


    sent_round(APPLIES - 2)
    sent_round(APPLIES - 1)
    for c in range(CHUNKS):
        store(c).wait()


def shards(source, link_blocks):
    src = pltpu.with_memory_space_constraint(source.reshape(NYX, DOF, RHS), pltpu.HBM)
    links = pltpu.with_memory_space_constraint(link_blocks.reshape(NYX, DIRS, DOF, DOF), pltpu.HBM)
    total = pl.pallas_call(
        kernel,
        out_shape=jax.ShapeDtypeStruct((NYX, DOF, RHS), jnp.float32),
        in_specs=[pl.BlockSpec(memory_space=pl.ANY)] * 2,
        out_specs=pl.BlockSpec(memory_space=pl.ANY),
        scratch_shapes=[
            pltpu.VMEM((NYX, DIRS, DOF, DOF), jnp.bfloat16),
            pltpu.VMEM((APPLIES, NYX, DOF, RHS), jnp.bfloat16),
            pltpu.VMEM((APPLIES, FACES, NYX, DOF, RHS), jnp.bfloat16),
            pltpu.VMEM((APPLIES, NYX, DOF, RHS), jnp.bfloat16),
            pltpu.VMEM((NYX, DOF, RHS), jnp.float32),
            pltpu.SemaphoreType.DMA((2,)),
            pltpu.SemaphoreType.DMA((APPLIES, FACES)),
            pltpu.SemaphoreType.DMA((APPLIES, FACES, CHUNKS)),
            pltpu.SemaphoreType.DMA((APPLIES, CHUNKS)),
            pltpu.SemaphoreType.DMA((APPLIES, 2)),
            pltpu.SemaphoreType.DMA((CHUNKS,)),
        ],
        compiler_params=pltpu.CompilerParams(
            collective_id=0, has_side_effects=True, vmem_limit_bytes=40 * 2**20
        ),
        cost_estimate=pl.CostEstimate(
            flops=2 * APPLIES * NYX * DIRS * DOF * DOF * RHS, bytes_accessed=6 * 2**20, transcendentals=0
        ),
    )(src, links)
    return total.reshape(1, 1, NYX, DOF, RHS)


def solution(mesh):
    placed = (P("ta", "gz", None, None, None), P("ta", "gz", None, None, None, None))
    return jax.shard_map(
        shards,
        mesh=mesh,
        in_specs=placed,
        out_specs=P("ta", "gz", None, None, None),
        check_vma=False,
    )
```

```python
import jax
import jax.numpy as jnp
from jax import lax
from jax.experimental import pallas as pl
from jax.experimental.pallas import tpu as pltpu
from jax.sharding import PartitionSpec as P

DOF = 96
DIRS = 9
RHS = 128
NX = 8
NY = 2
NYX = NX * NY
APPLIES = 4
CHUNK = 1
CHUNKS = NYX // CHUNK
STEPS = APPLIES * CHUNKS
DIRECT = CHUNKS
DIRECT_EDGE = 10
DIRECT_NEAR = 13
RELAY = CHUNKS
PASS = 9
FIRST = 4

FACES = 4
MESH = pl.DeviceIdType.MESH


def kernel(src, links_hbm, out, links, vecs, faces, relayed, summed, load_sem, send_sem, recv_sem, relay_sem, pass_sem, out_sem):
    t, z = lax.axis_index("ta"), lax.axis_index("gz")
    nt, nz = lax.axis_size("ta"), lax.axis_size("gz")
    half = nt // 2
    edge = lax.rem(t + 1, half) < 2
    near = jnp.logical_and(lax.rem(t + 2, half) < 4, jnp.logical_not(edge))
    inner = lax.rem(t + 2, half) >= 4
    high = t // half
    last = lax.rem(t, half) // (half - 1)
    partner = lax.rem(t + half, nt)

    z_out, z_out_face = lax.rem(z + high + (1 - high) * (nz - 1), nz), high
    z_over, z_over_face = lax.rem(z + (1 - high) + high * (nz - 1), nz), 1 - high
    t_in, t_in_face = lax.rem(t + (1 - last) + last * (nt - 1), nt), 3 - last
    t_over, t_over_face = lax.rem(t + last + (1 - last) * (nt - 1), nt), 2 + last
    t_pass = lax.rem(t_over + half, nt)

    load_links = pltpu.make_async_copy(links_hbm, links, load_sem.at[0])
    load_source = pltpu.make_async_copy(src, vecs.at[0], load_sem.at[1])
    load_source.start()
    load_links.start()

    barrier = pltpu.get_barrier_semaphore()

    def greet(target):
        pl.semaphore_signal(barrier, inc=1, device_id=target, device_id_type=MESH)

    greet((t, z_out))
    greet((t_in, z))
    greet((t, z_over))

    @pl.when(edge)
    def _():
        greet((partner, z))
        greet((partner, z_out))
        greet((t_pass, z))
        pl.semaphore_wait(barrier, 6)

    @pl.when(jnp.logical_not(edge))
    def _():
        greet((t_over, z))
        pl.semaphore_wait(barrier, 4)

    def remote(block, slot, send, recv, target):
        return pltpu.make_async_remote_copy(
            src_ref=block, dst_ref=slot, send_sem=send, recv_sem=recv, device_id=target, device_id_type=MESH
        )

    def part(c):
        return pl.ds(c * CHUNK, CHUNK)

    def push(block, k, c, face, target):
        remote(block, faces.at[k, face, part(c)], send_sem.at[k, face], recv_sem.at[k, face, c], target).start()

    def issue_relay(block, k, c):
        @pl.when(edge)
        def _():
            remote(
                block, relayed.at[k, part(c)], send_sem.at[k, z_over_face], relay_sem.at[k, c], (partner, z)
            ).start()

    def issue_edge(block, k, c):
        @pl.when(edge)
        def _():
            push(block, k, c, z_out_face, (t, z_out))
            push(block, k, c, t_in_face, (t_in, z))

    def push_all(block, k, c):
        push(block, k, c, z_out_face, (t, z_out))
        push(block, k, c, z_over_face, (t, z_over))
        push(block, k, c, t_over_face, (t_over, z))
        push(block, k, c, t_in_face, (t_in, z))

    def issue_near(block, k, c):
        @pl.when(near)
        def _():
            push_all(block, k, c)

    def issue_inner(block, k, c):
        @pl.when(inner)
        def _():
            push_all(block, k, c)

    def passed(k, c):
        block = relayed.at[k, part(c)]
        on_z = remote(
            block, faces.at[k, z_out_face, part(c)], pass_sem.at[k, 0], recv_sem.at[k, z_out_face, c], (partner, z_out)
        )
        on_t = remote(
            block, faces.at[k, t_over_face, part(c)], pass_sem.at[k, 1], recv_sem.at[k, t_over_face, c], (t_pass, z)
        )
        return on_z, on_t

    def issue_pass(k, c):
        @pl.when(edge)
        def _():
            remote(
                vecs.at[k, part(c)], relayed.at[k, part(c)], send_sem.at[k, 0], relay_sem.at[k, c], (partner, z)
            ).wait_recv()
            on_z, on_t = passed(k, c)
            on_z.start()
            on_t.start()

    def arrived(k, c):
        for face in range(FACES):
            remote(
                vecs.at[k, part(c)], faces.at[k, face, part(c)], send_sem.at[k, face], recv_sem.at[k, face, c], (t_in, z)
            ).wait_recv()

    def at_home(k, s):
        row, x = s // NX, lax.rem(s, NX)
        here = [
            s,
            row * NX + lax.rem(x + 1, NX),
            row * NX + lax.rem(x + NX - 1, NX),
            lax.rem(s + NX, NYX),
            lax.rem(s + NX, NYX),
        ]
        total = jnp.zeros((DOF, RHS), jnp.float32)
        for d, at in enumerate(here):
            total += jnp.dot(links[s, d], vecs[k, at], preferred_element_type=jnp.float32)
        return total

    def applied(k, c, store_site):
        sites = [c * CHUNK + i for i in range(CHUNK)]
        totals = [at_home(k, s) for s in sites]
        arrived(k, c)
        for s, total in zip(sites, totals):
            for face in range(FACES):
                total += jnp.dot(links[s, 5 + face], faces[k, face, s], preferred_element_type=jnp.float32)
            store_site(s, total)

    def whose(step):
        return step // CHUNKS, lax.rem(step, CHUNKS)

    def send(issue, step):
        k, c = whose(step)
        issue(vecs.at[k, part(c)], k, c)

    for c in range(CHUNKS):
        issue_relay(src.at[part(c)], 0, c)
        issue_inner(src.at[part(c)], 0, c)
        if c < DIRECT_NEAR:
            issue_near(src.at[part(c)], 0, c)
        if c < DIRECT_EDGE:
            issue_edge(src.at[part(c)], 0, c)
        if FIRST <= c < FIRST + PASS:
            issue_pass(0, c - FIRST)
    load_source.wait()
    load_links.wait()

    @pl.loop(0, STEPS - CHUNKS)
    def _(step):
        k, c = whose(step)

        def keep(s, total):
            vecs[k + 1, s] = total.astype(jnp.bfloat16)

        applied(k, c, keep)
        send(issue_edge, step + DIRECT_EDGE)
        send(issue_near, step + DIRECT_NEAR)
        send(issue_relay, step + RELAY)
        send(issue_inner, step + DIRECT)
        issue_pass(*whose(step + PASS))

    def sent(k, sem):
        remote(vecs.at[k], faces.at[k, 0], sem, recv_sem.at[k, 0, 0], (t_in, z)).wait_send()

    def sent_round(k):
        sent(k, send_sem.at[k, z_out_face])
        sent(k, send_sem.at[k, z_over_face])
        sent(k, send_sem.at[k, t_in_face])

        @pl.when(edge)
        def _():
            sent(k, pass_sem.at[k, 0])
            sent(k, pass_sem.at[k, 1])

        @pl.when(jnp.logical_not(edge))
        def _():
            sent(k, send_sem.at[k, t_over_face])

    for k in range(APPLIES - 2):
        sent_round(k)

    def store(c):
        return pltpu.make_async_copy(summed.at[part(c)], out.at[part(c)], out_sem.at[c])

    @pl.loop(0, CHUNKS)
    def _(c):
        def keep(s, total):
            summed[s] = total

        applied(APPLIES - 1, c, keep)
        store(c).start()

        @pl.when(c + DIRECT_NEAR < CHUNKS)
        def _():
            send(issue_near, STEPS - CHUNKS + c + DIRECT_NEAR)

        @pl.when(c + DIRECT_EDGE < CHUNKS)
        def _():
            send(issue_edge, STEPS - CHUNKS + c + DIRECT_EDGE)

        @pl.when(c + PASS < CHUNKS)
        def _():
            issue_pass(APPLIES - 1, c + PASS)


    sent_round(APPLIES - 2)
    sent_round(APPLIES - 1)
    for c in range(CHUNKS):
        store(c).wait()


def shards(source, link_blocks):
    src = pltpu.with_memory_space_constraint(source.reshape(NYX, DOF, RHS), pltpu.HBM)
    links = pltpu.with_memory_space_constraint(link_blocks.reshape(NYX, DIRS, DOF, DOF), pltpu.HBM)
    total = pl.pallas_call(
        kernel,
        out_shape=jax.ShapeDtypeStruct((NYX, DOF, RHS), jnp.float32),
        in_specs=[pl.BlockSpec(memory_space=pl.ANY)] * 2,
        out_specs=pl.BlockSpec(memory_space=pl.ANY),
        scratch_shapes=[
            pltpu.VMEM((NYX, DIRS, DOF, DOF), jnp.bfloat16),
            pltpu.VMEM((APPLIES, NYX, DOF, RHS), jnp.bfloat16),
            pltpu.VMEM((APPLIES, FACES, NYX, DOF, RHS), jnp.bfloat16),
            pltpu.VMEM((APPLIES, NYX, DOF, RHS), jnp.bfloat16),
            pltpu.VMEM((NYX, DOF, RHS), jnp.float32),
            pltpu.SemaphoreType.DMA((2,)),
            pltpu.SemaphoreType.DMA((APPLIES, FACES)),
            pltpu.SemaphoreType.DMA((APPLIES, FACES, CHUNKS)),
            pltpu.SemaphoreType.DMA((APPLIES, CHUNKS)),
            pltpu.SemaphoreType.DMA((APPLIES, 2)),
            pltpu.SemaphoreType.DMA((CHUNKS,)),
        ],
        compiler_params=pltpu.CompilerParams(
            collective_id=0, has_side_effects=True, vmem_limit_bytes=40 * 2**20
        ),
        cost_estimate=pl.CostEstimate(
            flops=2 * APPLIES * NYX * DIRS * DOF * DOF * RHS, bytes_accessed=6 * 2**20, transcendentals=0
        ),
    )(src, links)
    return total.reshape(1, 1, NYX, DOF, RHS)


def solution(mesh):
    placed = (P("ta", "gz", None, None, None), P("ta", "gz", None, None, None, None))
    return jax.shard_map(
        shards,
        mesh=mesh,
        in_specs=placed,
        out_specs=P("ta", "gz", None, None, None),
        check_vma=False,
    )
```

```python
import jax
import jax.numpy as jnp
from jax import lax
from jax.experimental import pallas as pl
from jax.experimental.pallas import tpu as pltpu
from jax.sharding import PartitionSpec as P

DOF = 96
DIRS = 9
RHS = 128
NX = 8
NY = 2
NYX = NX * NY
APPLIES = 4
CHUNK = 2
CHUNKS = NYX // CHUNK
STEPS = APPLIES * CHUNKS
DIRECT = CHUNKS
DIRECT_EDGE = 5
DIRECT_NEAR = 5
RELAY = CHUNKS
PASS = 5

FACES = 4
HOME = DIRS - FACES
MESH = pl.DeviceIdType.MESH


def kernel(src, links_hbm, out, links, home_links, face_links, vecs, faces, relayed, summed, load_sem, send_sem, recv_sem, relay_sem, pass_sem, out_sem):
    t, z = lax.axis_index("ta"), lax.axis_index("gz")
    nt, nz = lax.axis_size("ta"), lax.axis_size("gz")
    half = nt // 2
    edge = lax.rem(t + 1, half) < 2
    near = jnp.logical_and(lax.rem(t + 2, half) < 4, jnp.logical_not(edge))
    inner = lax.rem(t + 2, half) >= 4
    high = t // half
    last = lax.rem(t, half) // (half - 1)
    partner = lax.rem(t + half, nt)

    z_out, z_out_face = lax.rem(z + high + (1 - high) * (nz - 1), nz), high
    z_over, z_over_face = lax.rem(z + (1 - high) + high * (nz - 1), nz), 1 - high
    t_in, t_in_face = lax.rem(t + (1 - last) + last * (nt - 1), nt), 3 - last
    t_over, t_over_face = lax.rem(t + last + (1 - last) * (nt - 1), nt), 2 + last
    t_pass = lax.rem(t_over + half, nt)

    load_links = pltpu.make_async_copy(links_hbm, links, load_sem.at[0])
    load_source = pltpu.make_async_copy(src, vecs.at[0], load_sem.at[1])
    load_source.start()
    load_links.start()

    barrier = pltpu.get_barrier_semaphore()

    def greet(target):
        pl.semaphore_signal(barrier, inc=1, device_id=target, device_id_type=MESH)

    greet((t, z_out))
    greet((t_in, z))
    greet((t, z_over))

    @pl.when(edge)
    def _():
        greet((partner, z))
        greet((partner, z_out))
        greet((t_pass, z))
        pl.semaphore_wait(barrier, 6)

    @pl.when(jnp.logical_not(edge))
    def _():
        greet((t_over, z))
        pl.semaphore_wait(barrier, 4)

    def remote(block, slot, send, recv, target):
        return pltpu.make_async_remote_copy(
            src_ref=block, dst_ref=slot, send_sem=send, recv_sem=recv, device_id=target, device_id_type=MESH
        )

    def part(c):
        return pl.ds(c * CHUNK, CHUNK)

    def push(block, k, c, face, target):
        remote(block, faces.at[k, face, part(c)], send_sem.at[k, face], recv_sem.at[k, face, c], target).start()

    def issue_relay(block, k, c):
        @pl.when(edge)
        def _():
            remote(
                block, relayed.at[k, part(c)], send_sem.at[k, z_over_face], relay_sem.at[k, c], (partner, z)
            ).start()

    def issue_edge(block, k, c):
        @pl.when(edge)
        def _():
            push(block, k, c, z_out_face, (t, z_out))
            push(block, k, c, t_in_face, (t_in, z))

    def push_all(block, k, c):
        push(block, k, c, z_out_face, (t, z_out))
        push(block, k, c, z_over_face, (t, z_over))
        push(block, k, c, t_over_face, (t_over, z))
        push(block, k, c, t_in_face, (t_in, z))

    def issue_near(block, k, c):
        @pl.when(near)
        def _():
            push_all(block, k, c)

    def issue_inner(block, k, c):
        @pl.when(inner)
        def _():
            push_all(block, k, c)

    def passed(k, c):
        block = relayed.at[k, part(c)]
        on_z = remote(
            block, faces.at[k, z_out_face, part(c)], pass_sem.at[k, 0], recv_sem.at[k, z_out_face, c], (partner, z_out)
        )
        on_t = remote(
            block, faces.at[k, t_over_face, part(c)], pass_sem.at[k, 1], recv_sem.at[k, t_over_face, c], (t_pass, z)
        )
        return on_z, on_t

    def issue_pass(k, c):
        @pl.when(edge)
        def _():
            remote(
                vecs.at[k, part(c)], relayed.at[k, part(c)], send_sem.at[k, 0], relay_sem.at[k, c], (partner, z)
            ).wait_recv()
            on_z, on_t = passed(k, c)
            on_z.start()
            on_t.start()

    def arrived(k, c):
        for face in range(FACES):
            remote(
                vecs.at[k, part(c)], faces.at[k, face, part(c)], send_sem.at[k, face], recv_sem.at[k, face, c], (t_in, z)
            ).wait_recv()

    def at_home(k, s):
        row, x = s // NX, lax.rem(s, NX)
        here = [
            s,
            row * NX + lax.rem(x + 1, NX),
            row * NX + lax.rem(x + NX - 1, NX),
            lax.rem(s + NX, NYX),
            lax.rem(s + NX, NYX),
        ]
        stacked = jnp.concatenate([vecs[k, at] for at in here], axis=0)
        return jnp.dot(home_links[s], stacked, preferred_element_type=jnp.float32)

    def applied(k, c, store_site):
        sites = [c * CHUNK + i for i in range(CHUNK)]
        totals = [at_home(k, s) for s in sites]
        arrived(k, c)
        for s, total in zip(sites, totals):
            stacked = jnp.concatenate([faces[k, face, s] for face in range(FACES)], axis=0)
            total += jnp.dot(face_links[s], stacked, preferred_element_type=jnp.float32)
            store_site(s, total)

    def whose(step):
        return step // CHUNKS, lax.rem(step, CHUNKS)

    def send(issue, step):
        k, c = whose(step)
        issue(vecs.at[k, part(c)], k, c)

    for c in range(CHUNKS):
        issue_relay(src.at[part(c)], 0, c)
        issue_inner(src.at[part(c)], 0, c)
        if c < DIRECT_NEAR:
            issue_near(src.at[part(c)], 0, c)
        if c < DIRECT_EDGE:
            issue_edge(src.at[part(c)], 0, c)
        if c >= CHUNKS - PASS:
            issue_pass(0, c - (CHUNKS - PASS))
    load_source.wait()
    load_links.wait()

    @pl.loop(0, NYX)
    def _(s):
        home_links[s] = jnp.concatenate([links[s, d] for d in range(HOME)], axis=1)
        face_links[s] = jnp.concatenate([links[s, HOME + face] for face in range(FACES)], axis=1)

    @pl.loop(0, STEPS - CHUNKS)
    def _(step):
        k, c = whose(step)

        def keep(s, total):
            vecs[k + 1, s] = total.astype(jnp.bfloat16)

        applied(k, c, keep)
        send(issue_edge, step + DIRECT_EDGE)
        send(issue_near, step + DIRECT_NEAR)
        send(issue_relay, step + RELAY)
        send(issue_inner, step + DIRECT)
        issue_pass(*whose(step + PASS))

    def sent(k, sem):
        remote(vecs.at[k], faces.at[k, 0], sem, recv_sem.at[k, 0, 0], (t_in, z)).wait_send()

    def sent_round(k):
        sent(k, send_sem.at[k, z_out_face])
        sent(k, send_sem.at[k, z_over_face])
        sent(k, send_sem.at[k, t_in_face])

        @pl.when(edge)
        def _():
            sent(k, pass_sem.at[k, 0])
            sent(k, pass_sem.at[k, 1])

        @pl.when(jnp.logical_not(edge))
        def _():
            sent(k, send_sem.at[k, t_over_face])

    for k in range(APPLIES - 2):
        sent_round(k)

    def store(c):
        return pltpu.make_async_copy(summed.at[part(c)], out.at[part(c)], out_sem.at[c])

    @pl.loop(0, CHUNKS)
    def _(c):
        def keep(s, total):
            summed[s] = total

        applied(APPLIES - 1, c, keep)
        store(c).start()

        @pl.when(c + DIRECT_NEAR < CHUNKS)
        def _():
            send(issue_near, STEPS - CHUNKS + c + DIRECT_NEAR)

        @pl.when(c + DIRECT_EDGE < CHUNKS)
        def _():
            send(issue_edge, STEPS - CHUNKS + c + DIRECT_EDGE)

        @pl.when(c + PASS < CHUNKS)
        def _():
            issue_pass(APPLIES - 1, c + PASS)


    sent_round(APPLIES - 2)
    sent_round(APPLIES - 1)
    for c in range(CHUNKS):
        store(c).wait()


def shards(source, link_blocks):
    src = pltpu.with_memory_space_constraint(source.reshape(NYX, DOF, RHS), pltpu.HBM)
    links = pltpu.with_memory_space_constraint(link_blocks.reshape(NYX, DIRS, DOF, DOF), pltpu.HBM)
    total = pl.pallas_call(
        kernel,
        out_shape=jax.ShapeDtypeStruct((NYX, DOF, RHS), jnp.float32),
        in_specs=[pl.BlockSpec(memory_space=pl.ANY)] * 2,
        out_specs=pl.BlockSpec(memory_space=pl.ANY),
        scratch_shapes=[
            pltpu.VMEM((NYX, DIRS, DOF, DOF), jnp.bfloat16),
            pltpu.VMEM((NYX, DOF, HOME * DOF), jnp.bfloat16),
            pltpu.VMEM((NYX, DOF, FACES * DOF), jnp.bfloat16),
            pltpu.VMEM((APPLIES, NYX, DOF, RHS), jnp.bfloat16),
            pltpu.VMEM((APPLIES, FACES, NYX, DOF, RHS), jnp.bfloat16),
            pltpu.VMEM((APPLIES, NYX, DOF, RHS), jnp.bfloat16),
            pltpu.VMEM((NYX, DOF, RHS), jnp.float32),
            pltpu.SemaphoreType.DMA((2,)),
            pltpu.SemaphoreType.DMA((APPLIES, FACES)),
            pltpu.SemaphoreType.DMA((APPLIES, FACES, CHUNKS)),
            pltpu.SemaphoreType.DMA((APPLIES, CHUNKS)),
            pltpu.SemaphoreType.DMA((APPLIES, 2)),
            pltpu.SemaphoreType.DMA((CHUNKS,)),
        ],
        compiler_params=pltpu.CompilerParams(
            collective_id=0, has_side_effects=True, vmem_limit_bytes=40 * 2**20
        ),
        cost_estimate=pl.CostEstimate(
            flops=2 * APPLIES * NYX * DIRS * DOF * DOF * RHS, bytes_accessed=6 * 2**20, transcendentals=0
        ),
    )(src, links)
    return total.reshape(1, 1, NYX, DOF, RHS)


def solution(mesh):
    placed = (P("ta", "gz", None, None, None), P("ta", "gz", None, None, None, None))
    return jax.shard_map(
        shards,
        mesh=mesh,
        in_specs=placed,
        out_specs=P("ta", "gz", None, None, None),
        check_vma=False,
    )
```

```python
import jax
import jax.numpy as jnp
from jax import lax
from jax.experimental import pallas as pl
from jax.experimental.pallas import tpu as pltpu
from jax.sharding import PartitionSpec as P

DOF = 96
DIRS = 9
RHS = 128
NX = 8
NY = 2
NYX = NX * NY
APPLIES = 4
CHUNK = 2
CHUNKS = NYX // CHUNK
STEPS = APPLIES * CHUNKS
DIRECT = 6
DIRECT_EDGE = 5
DIRECT_STEP = 3
DIRECT_NEAR = 5
RELAY = CHUNKS
PASS = 4

FACES = 4
MESH = pl.DeviceIdType.MESH


def kernel(src, links_hbm, out, links, vecs, faces, relayed, summed, load_sem, send_sem, recv_sem, relay_sem, pass_sem, out_sem):
    t, z = lax.axis_index("ta"), lax.axis_index("gz")
    nt, nz = lax.axis_size("ta"), lax.axis_size("gz")
    half = nt // 2
    edge = lax.rem(t + 1, half) < 2
    near = jnp.logical_and(lax.rem(t + 2, half) < 4, jnp.logical_not(edge))
    inner = lax.rem(t + 2, half) >= 4
    high = t // half
    last = lax.rem(t, half) // (half - 1)
    partner = lax.rem(t + half, nt)

    z_out, z_out_face = lax.rem(z + high + (1 - high) * (nz - 1), nz), high
    z_over, z_over_face = lax.rem(z + (1 - high) + high * (nz - 1), nz), 1 - high
    t_in, t_in_face = lax.rem(t + (1 - last) + last * (nt - 1), nt), 3 - last
    t_over, t_over_face = lax.rem(t + last + (1 - last) * (nt - 1), nt), 2 + last
    t_pass = lax.rem(t_over + half, nt)

    load_links = pltpu.make_async_copy(links_hbm, links, load_sem.at[0])
    load_source = pltpu.make_async_copy(src, vecs.at[0], load_sem.at[1])
    load_source.start()
    load_links.start()

    barrier = pltpu.get_barrier_semaphore()

    def greet(target):
        pl.semaphore_signal(barrier, inc=1, device_id=target, device_id_type=MESH)

    greet((t, z_out))
    greet((t_in, z))
    greet((t, z_over))

    @pl.when(edge)
    def _():
        greet((partner, z))
        greet((partner, z_out))
        greet((t_pass, z))
        pl.semaphore_wait(barrier, 6)

    @pl.when(jnp.logical_not(edge))
    def _():
        greet((t_over, z))
        pl.semaphore_wait(barrier, 4)

    def remote(block, slot, send, recv, target):
        return pltpu.make_async_remote_copy(
            src_ref=block, dst_ref=slot, send_sem=send, recv_sem=recv, device_id=target, device_id_type=MESH
        )

    def part(c):
        return pl.ds(c * CHUNK, CHUNK)

    def push(block, k, c, face, target):
        remote(block, faces.at[k, face, part(c)], send_sem.at[k, face], recv_sem.at[k, face, c], target).start()

    def issue_relay(block, k, c):
        @pl.when(edge)
        def _():
            remote(
                block, relayed.at[k, part(c)], send_sem.at[k, z_over_face], relay_sem.at[k, c], (partner, z)
            ).start()

    def issue_edge(block, k, c):
        @pl.when(edge)
        def _():
            push(block, k, c, z_out_face, (t, z_out))

    def issue_edge_in(block, k, c):
        @pl.when(edge)
        def _():
            push(block, k, c, t_in_face, (t_in, z))

    def push_all(block, k, c):
        push(block, k, c, z_out_face, (t, z_out))
        push(block, k, c, z_over_face, (t, z_over))
        push(block, k, c, t_over_face, (t_over, z))
        push(block, k, c, t_in_face, (t_in, z))

    def issue_near(block, k, c):
        @pl.when(near)
        def _():
            push_all(block, k, c)

    def issue_inner(block, k, c):
        @pl.when(inner)
        def _():
            push_all(block, k, c)

    def passed(k, c):
        block = relayed.at[k, part(c)]
        on_z = remote(
            block, faces.at[k, z_out_face, part(c)], pass_sem.at[k, 0], recv_sem.at[k, z_out_face, c], (partner, z_out)
        )
        on_t = remote(
            block, faces.at[k, t_over_face, part(c)], pass_sem.at[k, 1], recv_sem.at[k, t_over_face, c], (t_pass, z)
        )
        return on_z, on_t

    def issue_pass(k, c):
        @pl.when(edge)
        def _():
            remote(
                vecs.at[k, part(c)], relayed.at[k, part(c)], send_sem.at[k, 0], relay_sem.at[k, c], (partner, z)
            ).wait_recv()
            on_z, on_t = passed(k, c)
            on_z.start()
            on_t.start()

    def arrived(k, c):
        for face in range(FACES):
            remote(
                vecs.at[k, part(c)], faces.at[k, face, part(c)], send_sem.at[k, face], recv_sem.at[k, face, c], (t_in, z)
            ).wait_recv()

    def at_home(k, s):
        row, x = s // NX, lax.rem(s, NX)
        here = [
            s,
            row * NX + lax.rem(x + 1, NX),
            row * NX + lax.rem(x + NX - 1, NX),
            lax.rem(s + NX, NYX),
            lax.rem(s + NX, NYX),
        ]
        total = jnp.zeros((DOF, RHS), jnp.float32)
        for d, at in enumerate(here):
            total += jnp.dot(links[s, d], vecs[k, at], preferred_element_type=jnp.float32)
        return total

    def applied(k, c, store_site):
        sites = [c * CHUNK + i for i in range(CHUNK)]
        totals = [at_home(k, s) for s in sites]
        arrived(k, c)
        for s, total in zip(sites, totals):
            for face in range(FACES):
                total += jnp.dot(links[s, 5 + face], faces[k, face, s], preferred_element_type=jnp.float32)
            store_site(s, total)

    def whose(step):
        return step // CHUNKS, lax.rem(step, CHUNKS)

    def send(issue, step):
        k, c = whose(step)
        issue(vecs.at[k, part(c)], k, c)

    windows = [
        (issue_inner, DIRECT),
        (issue_near, DIRECT_NEAR),
        (issue_edge, DIRECT_EDGE),
        (issue_edge_in, DIRECT_STEP),
    ]

    for c in range(CHUNKS):
        issue_relay(src.at[part(c)], 0, c)
        for issue, ahead in windows:
            if c < ahead:
                issue(src.at[part(c)], 0, c)
        if c >= CHUNKS - PASS:
            issue_pass(0, c - (CHUNKS - PASS))
    load_source.wait()
    load_links.wait()

    @pl.loop(0, STEPS - CHUNKS)
    def _(step):
        k, c = whose(step)

        def keep(s, total):
            vecs[k + 1, s] = total.astype(jnp.bfloat16)

        applied(k, c, keep)
        for issue, ahead in windows:
            send(issue, step + ahead)
        send(issue_relay, step + RELAY)
        issue_pass(*whose(step + PASS))

    def sent(k, sem):
        remote(vecs.at[k], faces.at[k, 0], sem, recv_sem.at[k, 0, 0], (t_in, z)).wait_send()

    def sent_round(k):
        sent(k, send_sem.at[k, z_out_face])
        sent(k, send_sem.at[k, z_over_face])
        sent(k, send_sem.at[k, t_in_face])

        @pl.when(edge)
        def _():
            sent(k, pass_sem.at[k, 0])
            sent(k, pass_sem.at[k, 1])

        @pl.when(jnp.logical_not(edge))
        def _():
            sent(k, send_sem.at[k, t_over_face])

    for k in range(APPLIES - 2):
        sent_round(k)

    def store(c):
        return pltpu.make_async_copy(summed.at[part(c)], out.at[part(c)], out_sem.at[c])

    @pl.loop(0, CHUNKS)
    def _(c):
        def keep(s, total):
            summed[s] = total

        applied(APPLIES - 1, c, keep)
        store(c).start()

        for issue, ahead in windows:

            @pl.when(c + ahead < CHUNKS)
            def _():
                send(issue, STEPS - CHUNKS + c + ahead)

        @pl.when(c + PASS < CHUNKS)
        def _():
            issue_pass(APPLIES - 1, c + PASS)


    sent_round(APPLIES - 2)
    sent_round(APPLIES - 1)
    for c in range(CHUNKS):
        store(c).wait()


def shards(source, link_blocks):
    src = pltpu.with_memory_space_constraint(source.reshape(NYX, DOF, RHS), pltpu.HBM)
    links = pltpu.with_memory_space_constraint(link_blocks.reshape(NYX, DIRS, DOF, DOF), pltpu.HBM)
    total = pl.pallas_call(
        kernel,
        out_shape=jax.ShapeDtypeStruct((NYX, DOF, RHS), jnp.float32),
        in_specs=[pl.BlockSpec(memory_space=pl.ANY)] * 2,
        out_specs=pl.BlockSpec(memory_space=pl.ANY),
        scratch_shapes=[
            pltpu.VMEM((NYX, DIRS, DOF, DOF), jnp.bfloat16),
            pltpu.VMEM((APPLIES, NYX, DOF, RHS), jnp.bfloat16),
            pltpu.VMEM((APPLIES, FACES, NYX, DOF, RHS), jnp.bfloat16),
            pltpu.VMEM((APPLIES, NYX, DOF, RHS), jnp.bfloat16),
            pltpu.VMEM((NYX, DOF, RHS), jnp.float32),
            pltpu.SemaphoreType.DMA((2,)),
            pltpu.SemaphoreType.DMA((APPLIES, FACES)),
            pltpu.SemaphoreType.DMA((APPLIES, FACES, CHUNKS)),
            pltpu.SemaphoreType.DMA((APPLIES, CHUNKS)),
            pltpu.SemaphoreType.DMA((APPLIES, 2)),
            pltpu.SemaphoreType.DMA((CHUNKS,)),
        ],
        compiler_params=pltpu.CompilerParams(
            collective_id=0, has_side_effects=True, vmem_limit_bytes=40 * 2**20
        ),
        cost_estimate=pl.CostEstimate(
            flops=2 * APPLIES * NYX * DIRS * DOF * DOF * RHS, bytes_accessed=6 * 2**20, transcendentals=0
        ),
    )(src, links)
    return total.reshape(1, 1, NYX, DOF, RHS)


def solution(mesh):
    placed = (P("ta", "gz", None, None, None), P("ta", "gz", None, None, None, None))
    return jax.shard_map(
        shards,
        mesh=mesh,
        in_specs=placed,
        out_specs=P("ta", "gz", None, None, None),
        check_vma=False,
    )
```

```python
import jax
import jax.numpy as jnp
from jax import lax
from jax.experimental import pallas as pl
from jax.experimental.pallas import tpu as pltpu
from jax.sharding import PartitionSpec as P

DOF = 96
DIRS = 9
RHS = 128
NX = 8
NY = 2
NYX = NX * NY
APPLIES = 4
CHUNK = 2
CHUNKS = NYX // CHUNK
STEPS = APPLIES * CHUNKS
DIRECT_EDGE = 5
DIRECT_NEAR = 6
DIRECT = 6
RELAY = CHUNKS
PASS = 5

FACES = 4
MESH = pl.DeviceIdType.MESH


def kernel(src, links_hbm, out, links, vecs, faces, relayed, summed, load_sem, send_sem, recv_sem, relay_sem, pass_sem, out_sem):
    t, z = lax.axis_index("ta"), lax.axis_index("gz")
    nt, nz = lax.axis_size("ta"), lax.axis_size("gz")
    half = nt // 2
    edge = lax.rem(t + 1, half) < 2
    off_edge = (lax.rem(t + 1, half) // 2 + half // 2 - 1) // (half // 2)
    near = jnp.logical_and(lax.rem(t + 2, half) < 4, jnp.logical_not(edge))
    inner = lax.rem(t + 2, half) >= 4
    high = t // half
    last = lax.rem(t, half) // (half // 2)

    z_out, z_out_face = lax.rem(z + high + (1 - high) * (nz - 1), nz), high
    z_over, z_over_face = lax.rem(z + (1 - high) + high * (nz - 1), nz), 1 - high
    t_in, t_in_face = lax.rem(t + (1 - last) + last * (nt - 1), nt), 3 - last
    t_over, t_over_face = lax.rem(t + last + (1 - last) * (nt - 1), nt), 2 + last
    own_edge = t + off_edge * (2 * last - 1)
    partner = lax.rem(own_edge + half, nt)
    partner_near = partner + 1 - 2 * last
    t_pass = lax.rem(own_edge + last + (1 - last) * (nt - 1) + half, nt)
    t_pass_near = t_pass - 1 + 2 * last

    load_links = pltpu.make_async_copy(links_hbm, links, load_sem.at[0])
    load_source = pltpu.make_async_copy(src, vecs.at[0], load_sem.at[1])
    load_source.start()
    load_links.start()

    barrier = pltpu.get_barrier_semaphore()

    def greet(target):
        pl.semaphore_signal(barrier, inc=1, device_id=target, device_id_type=MESH)

    greet((t, z_out))
    greet((t_in, z))
    greet((t, z_over))

    @pl.when(jnp.logical_not(inner))
    def _():
        greet((partner, z))
        greet((partner, z_out))
        greet((t_pass, z))

    @pl.when(edge)
    def _():
        greet((partner_near, z))
        greet((partner_near, z_out))
        greet((t_pass_near, z))
        pl.semaphore_wait(barrier, 9)

    @pl.when(near)
    def _():
        greet((t_over, z))
        pl.semaphore_wait(barrier, 7)

    @pl.when(inner)
    def _():
        greet((t_over, z))
        pl.semaphore_wait(barrier, 4)

    def remote(block, slot, send, recv, target):
        return pltpu.make_async_remote_copy(
            src_ref=block, dst_ref=slot, send_sem=send, recv_sem=recv, device_id=target, device_id_type=MESH
        )

    def part(c):
        return pl.ds(c * CHUNK, CHUNK)

    def push(block, k, c, face, target):
        remote(block, faces.at[k, face, part(c)], send_sem.at[k, face], recv_sem.at[k, face, c], target).start()

    def issue_relay(block, k, c):
        @pl.when(edge)
        def _():
            remote(
                block,
                relayed.at[k, part(c)],
                send_sem.at[k, z_over_face],
                relay_sem.at[k, c],
                (partner + lax.rem(c, 2) * (partner_near - partner), z),
            ).start()

    def issue_edge(block, k, c):
        @pl.when(edge)
        def _():
            push(block, k, c, z_out_face, (t, z_out))
            push(block, k, c, t_in_face, (t_in, z))

    def push_all(block, k, c):
        push(block, k, c, z_out_face, (t, z_out))
        push(block, k, c, z_over_face, (t, z_over))
        push(block, k, c, t_over_face, (t_over, z))
        push(block, k, c, t_in_face, (t_in, z))

    def issue_near(block, k, c):
        @pl.when(near)
        def _():
            push_all(block, k, c)

    def issue_inner(block, k, c):
        @pl.when(inner)
        def _():
            push_all(block, k, c)

    def passed(k, c):
        block = relayed.at[k, part(c)]
        on_z = remote(
            block, faces.at[k, z_out_face, part(c)], pass_sem.at[k, 0], recv_sem.at[k, z_out_face, c], (partner, z_out)
        )
        on_t = remote(
            block, faces.at[k, t_over_face, part(c)], pass_sem.at[k, 1], recv_sem.at[k, t_over_face, c], (t_pass, z)
        )
        return on_z, on_t

    def issue_pass(k, c):
        odd = lax.rem(c, 2) == 1

        @pl.when(jnp.logical_or(jnp.logical_and(edge, jnp.logical_not(odd)), jnp.logical_and(near, odd)))
        def _():
            remote(
                vecs.at[k, part(c)], relayed.at[k, part(c)], send_sem.at[k, 0], relay_sem.at[k, c], (partner, z)
            ).wait_recv()
            on_z, on_t = passed(k, c)
            on_z.start()
            on_t.start()

    def arrived(k, c):
        for face in range(FACES):
            remote(
                vecs.at[k, part(c)], faces.at[k, face, part(c)], send_sem.at[k, face], recv_sem.at[k, face, c], (t_in, z)
            ).wait_recv()

    def at_home(k, s):
        row, x = s // NX, lax.rem(s, NX)
        here = [
            s,
            row * NX + lax.rem(x + 1, NX),
            row * NX + lax.rem(x + NX - 1, NX),
            lax.rem(s + NX, NYX),
            lax.rem(s + NX, NYX),
        ]
        total = jnp.zeros((DOF, RHS), jnp.float32)
        for d, at in enumerate(here):
            total += jnp.dot(links[s, d], vecs[k, at], preferred_element_type=jnp.float32)
        return total

    def applied(k, c, store_site):
        sites = [c * CHUNK + i for i in range(CHUNK)]
        totals = [at_home(k, s) for s in sites]
        arrived(k, c)
        for s, total in zip(sites, totals):
            for face in range(FACES):
                total += jnp.dot(links[s, 5 + face], faces[k, face, s], preferred_element_type=jnp.float32)
            store_site(s, total)

    def whose(step):
        return step // CHUNKS, lax.rem(step, CHUNKS)

    def send(issue, step):
        k, c = whose(step)
        issue(vecs.at[k, part(c)], k, c)

    windows = [
        (issue_inner, DIRECT),
        (issue_near, DIRECT_NEAR),
        (issue_edge, DIRECT_EDGE),
    ]

    for c in range(CHUNKS):
        issue_relay(src.at[part(c)], 0, jnp.int32(c))
        for issue, ahead in windows:
            if c < ahead:
                issue(src.at[part(c)], 0, c)
        if c >= CHUNKS - PASS:
            issue_pass(0, jnp.int32(c - (CHUNKS - PASS)))
    load_source.wait()
    load_links.wait()

    @pl.loop(0, STEPS - CHUNKS)
    def _(step):
        k, c = whose(step)

        def keep(s, total):
            vecs[k + 1, s] = total.astype(jnp.bfloat16)

        applied(k, c, keep)
        for issue, ahead in windows:
            send(issue, step + ahead)
        send(issue_relay, step + RELAY)
        issue_pass(*whose(step + PASS))

    def sent(k, sem, sites=NYX):
        block = pl.ds(0, sites)
        remote(vecs.at[k, block], faces.at[k, 0, block], sem, recv_sem.at[k, 0, 0], (t_in, z)).wait_send()

    def sent_round(k):
        sent(k, send_sem.at[k, z_out_face])
        sent(k, send_sem.at[k, z_over_face])
        sent(k, send_sem.at[k, t_in_face])

        @pl.when(jnp.logical_not(inner))
        def _():
            sent(k, pass_sem.at[k, 0], NYX // 2)
            sent(k, pass_sem.at[k, 1], NYX // 2)

        @pl.when(jnp.logical_not(edge))
        def _():
            sent(k, send_sem.at[k, t_over_face])

    for k in range(APPLIES - 2):
        sent_round(k)

    def store(c):
        return pltpu.make_async_copy(summed.at[part(c)], out.at[part(c)], out_sem.at[c])

    @pl.loop(0, CHUNKS)
    def _(c):
        def keep(s, total):
            summed[s] = total

        applied(APPLIES - 1, c, keep)
        store(c).start()

        for issue, ahead in windows:

            @pl.when(c + ahead < CHUNKS)
            def _():
                send(issue, STEPS - CHUNKS + c + ahead)

        @pl.when(c + PASS < CHUNKS)
        def _():
            issue_pass(APPLIES - 1, c + PASS)


    sent_round(APPLIES - 2)
    sent_round(APPLIES - 1)
    for c in range(CHUNKS):
        store(c).wait()


def shards(source, link_blocks):
    src = pltpu.with_memory_space_constraint(source.reshape(NYX, DOF, RHS), pltpu.HBM)
    links = pltpu.with_memory_space_constraint(link_blocks.reshape(NYX, DIRS, DOF, DOF), pltpu.HBM)
    total = pl.pallas_call(
        kernel,
        out_shape=jax.ShapeDtypeStruct((NYX, DOF, RHS), jnp.float32),
        in_specs=[pl.BlockSpec(memory_space=pl.ANY)] * 2,
        out_specs=pl.BlockSpec(memory_space=pl.ANY),
        scratch_shapes=[
            pltpu.VMEM((NYX, DIRS, DOF, DOF), jnp.bfloat16),
            pltpu.VMEM((APPLIES, NYX, DOF, RHS), jnp.bfloat16),
            pltpu.VMEM((APPLIES, FACES, NYX, DOF, RHS), jnp.bfloat16),
            pltpu.VMEM((APPLIES, NYX, DOF, RHS), jnp.bfloat16),
            pltpu.VMEM((NYX, DOF, RHS), jnp.float32),
            pltpu.SemaphoreType.DMA((2,)),
            pltpu.SemaphoreType.DMA((APPLIES, FACES)),
            pltpu.SemaphoreType.DMA((APPLIES, FACES, CHUNKS)),
            pltpu.SemaphoreType.DMA((APPLIES, CHUNKS)),
            pltpu.SemaphoreType.DMA((APPLIES, 2)),
            pltpu.SemaphoreType.DMA((CHUNKS,)),
        ],
        compiler_params=pltpu.CompilerParams(
            collective_id=0, has_side_effects=True, vmem_limit_bytes=40 * 2**20
        ),
        cost_estimate=pl.CostEstimate(
            flops=2 * APPLIES * NYX * DIRS * DOF * DOF * RHS, bytes_accessed=6 * 2**20, transcendentals=0
        ),
    )(src, links)
    return total.reshape(1, 1, NYX, DOF, RHS)


def solution(mesh):
    placed = (P("ta", "gz", None, None, None), P("ta", "gz", None, None, None, None))
    return jax.shard_map(
        shards,
        mesh=mesh,
        in_specs=placed,
        out_specs=P("ta", "gz", None, None, None),
        check_vma=False,
    )
```

```python
import jax
import jax.numpy as jnp
from jax import lax
from jax.experimental import pallas as pl
from jax.experimental.pallas import tpu as pltpu
from jax.sharding import PartitionSpec as P

DOF = 96
DIRS = 9
RHS = 128
NX = 8
NY = 2
NYX = NX * NY
APPLIES = 4
CHUNK = 2
CHUNKS = NYX // CHUNK
STEPS = APPLIES * CHUNKS
DIRECT_EDGE = 5
DIRECT_NEAR = 6
DIRECT = 6
RELAY = CHUNKS
PASS = 5

FACES = 4
MESH = pl.DeviceIdType.MESH


def kernel(src, links_hbm, out, links, vecs, faces, relayed, summed, load_sem, send_sem, recv_sem, relay_sem, pass_sem, out_sem):
    t, z = lax.axis_index("ta"), lax.axis_index("gz")
    nt, nz = lax.axis_size("ta"), lax.axis_size("gz")
    half = nt // 2
    edge = lax.rem(t + 1, half) < 2
    off_edge = (lax.rem(t + 1, half) // 2 + half // 2 - 1) // (half // 2)
    near = jnp.logical_and(lax.rem(t + 2, half) < 4, jnp.logical_not(edge))
    inner = lax.rem(t + 2, half) >= 4
    high = t // half
    last = lax.rem(t, half) // (half // 2)

    z_out, z_out_face = lax.rem(z + high + (1 - high) * (nz - 1), nz), high
    z_over, z_over_face = lax.rem(z + (1 - high) + high * (nz - 1), nz), 1 - high
    t_in, t_in_face = lax.rem(t + (1 - last) + last * (nt - 1), nt), 3 - last
    t_over, t_over_face = lax.rem(t + last + (1 - last) * (nt - 1), nt), 2 + last
    own_edge = t + off_edge * (2 * last - 1)
    partner = lax.rem(own_edge + half, nt)
    partner_near = partner + 1 - 2 * last
    t_pass = lax.rem(own_edge + last + (1 - last) * (nt - 1) + half, nt)
    t_pass_near = t_pass - 1 + 2 * last

    load_links = pltpu.make_async_copy(links_hbm, links, load_sem.at[0])
    load_source = pltpu.make_async_copy(src, vecs.at[0], load_sem.at[1])

    barrier = pltpu.get_barrier_semaphore()

    def greet(target):
        pl.semaphore_signal(barrier, inc=1, device_id=target, device_id_type=MESH)

    greet((t, z_out))
    greet((t_in, z))
    greet((t, z_over))
    load_source.start(priority=1)

    @pl.when(jnp.logical_not(inner))
    def _():
        greet((partner, z))
        greet((partner, z_out))
        greet((t_pass, z))

    @pl.when(edge)
    def _():
        greet((partner_near, z))
        greet((partner_near, z_out))
        greet((t_pass_near, z))
        pl.semaphore_wait(barrier, 9)

    @pl.when(near)
    def _():
        greet((t_over, z))
        pl.semaphore_wait(barrier, 7)

    @pl.when(inner)
    def _():
        greet((t_over, z))
        pl.semaphore_wait(barrier, 4)

    def remote(block, slot, send, recv, target):
        return pltpu.make_async_remote_copy(
            src_ref=block, dst_ref=slot, send_sem=send, recv_sem=recv, device_id=target, device_id_type=MESH
        )

    def part(c):
        return pl.ds(c * CHUNK, CHUNK)

    def push(block, k, c, face, target):
        remote(block, faces.at[k, face, part(c)], send_sem.at[k, face], recv_sem.at[k, face, c], target).start()

    def issue_relay(block, k, c):
        @pl.when(edge)
        def _():
            remote(
                block,
                relayed.at[k, part(c)],
                send_sem.at[k, z_over_face],
                relay_sem.at[k, c],
                (partner + lax.rem(c, 2) * (partner_near - partner), z),
            ).start()

    def issue_edge(block, k, c):
        @pl.when(edge)
        def _():
            push(block, k, c, z_out_face, (t, z_out))
            push(block, k, c, t_in_face, (t_in, z))

    def push_all(block, k, c):
        push(block, k, c, z_out_face, (t, z_out))
        push(block, k, c, z_over_face, (t, z_over))
        push(block, k, c, t_over_face, (t_over, z))
        push(block, k, c, t_in_face, (t_in, z))

    def issue_near(block, k, c):
        @pl.when(near)
        def _():
            push_all(block, k, c)

    def issue_inner(block, k, c):
        @pl.when(inner)
        def _():
            push_all(block, k, c)

    def passed(k, c):
        block = relayed.at[k, part(c)]
        on_z = remote(
            block, faces.at[k, z_out_face, part(c)], pass_sem.at[k, 0], recv_sem.at[k, z_out_face, c], (partner, z_out)
        )
        on_t = remote(
            block, faces.at[k, t_over_face, part(c)], pass_sem.at[k, 1], recv_sem.at[k, t_over_face, c], (t_pass, z)
        )
        return on_z, on_t

    def issue_pass(k, c):
        odd = lax.rem(c, 2) == 1

        @pl.when(jnp.logical_or(jnp.logical_and(edge, jnp.logical_not(odd)), jnp.logical_and(near, odd)))
        def _():
            remote(
                vecs.at[k, part(c)], relayed.at[k, part(c)], send_sem.at[k, 0], relay_sem.at[k, c], (partner, z)
            ).wait_recv()
            on_z, on_t = passed(k, c)
            on_z.start()
            on_t.start()

    def arrived(k, c):
        for face in range(FACES):
            remote(
                vecs.at[k, part(c)], faces.at[k, face, part(c)], send_sem.at[k, face], recv_sem.at[k, face, c], (t_in, z)
            ).wait_recv()

    def at_home(k, s):
        row, x = s // NX, lax.rem(s, NX)
        here = [
            s,
            row * NX + lax.rem(x + 1, NX),
            row * NX + lax.rem(x + NX - 1, NX),
            lax.rem(s + NX, NYX),
            lax.rem(s + NX, NYX),
        ]
        total = jnp.zeros((DOF, RHS), jnp.float32)
        for d, at in enumerate(here):
            total += jnp.dot(links[s, d], vecs[k, at], preferred_element_type=jnp.float32)
        return total

    def applied(k, c, store_site):
        sites = [c * CHUNK + i for i in range(CHUNK)]
        totals = [at_home(k, s) for s in sites]
        arrived(k, c)
        for s, total in zip(sites, totals):
            for face in range(FACES):
                total += jnp.dot(links[s, 5 + face], faces[k, face, s], preferred_element_type=jnp.float32)
            store_site(s, total)

    def whose(step):
        return step // CHUNKS, lax.rem(step, CHUNKS)

    def send(issue, step):
        k, c = whose(step)
        issue(vecs.at[k, part(c)], k, c)

    windows = [
        (issue_inner, DIRECT),
        (issue_near, DIRECT_NEAR),
        (issue_edge, DIRECT_EDGE),
    ]

    for c in range(CHUNKS):
        issue_relay(src.at[part(c)], 0, jnp.int32(c))
        for issue, ahead in windows:
            if c < ahead:
                issue(src.at[part(c)], 0, c)
        if c == 1:
            load_links.start(priority=1)
        if c >= CHUNKS - PASS:
            issue_pass(0, jnp.int32(c - (CHUNKS - PASS)))
    load_source.wait()
    load_links.wait()

    @pl.loop(0, STEPS - CHUNKS)
    def _(step):
        k, c = whose(step)

        def keep(s, total):
            vecs[k + 1, s] = total.astype(jnp.bfloat16)

        applied(k, c, keep)
        for issue, ahead in windows:
            send(issue, step + ahead)
        send(issue_relay, step + RELAY)
        issue_pass(*whose(step + PASS))

    def sent(k, sem, sites=NYX):
        block = pl.ds(0, sites)
        remote(vecs.at[k, block], faces.at[k, 0, block], sem, recv_sem.at[k, 0, 0], (t_in, z)).wait_send()

    def sent_round(k):
        sent(k, send_sem.at[k, z_out_face])
        sent(k, send_sem.at[k, z_over_face])
        sent(k, send_sem.at[k, t_in_face])

        @pl.when(jnp.logical_not(inner))
        def _():
            sent(k, pass_sem.at[k, 0], NYX // 2)
            sent(k, pass_sem.at[k, 1], NYX // 2)

        @pl.when(jnp.logical_not(edge))
        def _():
            sent(k, send_sem.at[k, t_over_face])

    for k in range(APPLIES - 2):
        sent_round(k)

    def store(c):
        return pltpu.make_async_copy(summed.at[part(c)], out.at[part(c)], out_sem.at[c])

    @pl.loop(0, CHUNKS)
    def _(c):
        def keep(s, total):
            summed[s] = total

        applied(APPLIES - 1, c, keep)
        store(c).start()

        for issue, ahead in windows:

            @pl.when(c + ahead < CHUNKS)
            def _():
                send(issue, STEPS - CHUNKS + c + ahead)

        @pl.when(c + PASS < CHUNKS)
        def _():
            issue_pass(APPLIES - 1, c + PASS)


    sent_round(APPLIES - 2)
    sent_round(APPLIES - 1)
    for c in range(CHUNKS):
        store(c).wait()


def shards(source, link_blocks):
    src = pltpu.with_memory_space_constraint(source.reshape(NYX, DOF, RHS), pltpu.HBM)
    links = pltpu.with_memory_space_constraint(link_blocks.reshape(NYX, DIRS, DOF, DOF), pltpu.HBM)
    total = pl.pallas_call(
        kernel,
        out_shape=jax.ShapeDtypeStruct((NYX, DOF, RHS), jnp.float32),
        in_specs=[pl.BlockSpec(memory_space=pl.ANY)] * 2,
        out_specs=pl.BlockSpec(memory_space=pl.ANY),
        scratch_shapes=[
            pltpu.VMEM((NYX, DIRS, DOF, DOF), jnp.bfloat16),
            pltpu.VMEM((APPLIES, NYX, DOF, RHS), jnp.bfloat16),
            pltpu.VMEM((APPLIES, FACES, NYX, DOF, RHS), jnp.bfloat16),
            pltpu.VMEM((APPLIES, NYX, DOF, RHS), jnp.bfloat16),
            pltpu.VMEM((NYX, DOF, RHS), jnp.float32),
            pltpu.SemaphoreType.DMA((2,)),
            pltpu.SemaphoreType.DMA((APPLIES, FACES)),
            pltpu.SemaphoreType.DMA((APPLIES, FACES, CHUNKS)),
            pltpu.SemaphoreType.DMA((APPLIES, CHUNKS)),
            pltpu.SemaphoreType.DMA((APPLIES, 2)),
            pltpu.SemaphoreType.DMA((CHUNKS,)),
        ],
        compiler_params=pltpu.CompilerParams(
            collective_id=0, has_side_effects=True, vmem_limit_bytes=40 * 2**20
        ),
        cost_estimate=pl.CostEstimate(
            flops=2 * APPLIES * NYX * DIRS * DOF * DOF * RHS, bytes_accessed=6 * 2**20, transcendentals=0
        ),
    )(src, links)
    return total.reshape(1, 1, NYX, DOF, RHS)


def solution(mesh):
    placed = (P("ta", "gz", None, None, None), P("ta", "gz", None, None, None, None))
    return jax.shard_map(
        shards,
        mesh=mesh,
        in_specs=placed,
        out_specs=P("ta", "gz", None, None, None),
        check_vma=False,
    )
```

```python
import jax
import jax.numpy as jnp
from jax import lax
from jax.experimental import pallas as pl
from jax.experimental.pallas import tpu as pltpu
from jax.sharding import PartitionSpec as P

DOF = 96
DIRS = 9
RHS = 128
NX = 8
NY = 2
NYX = NX * NY
APPLIES = 4
CHUNK = 2
CHUNKS = NYX // CHUNK
STEPS = APPLIES * CHUNKS
DIRECT_EDGE = 5
DIRECT_NEAR = CHUNKS
DIRECT = CHUNKS
RELAY = CHUNKS
PASS = 4

FACES = 4
MESH = pl.DeviceIdType.MESH


def kernel(src, links_hbm, out, links, vecs, faces, relayed, summed, load_sem, send_sem, recv_sem, relay_sem, pass_sem, out_sem):
    t, z = lax.axis_index("ta"), lax.axis_index("gz")
    nt, nz = lax.axis_size("ta"), lax.axis_size("gz")
    half = nt // 2
    edge = lax.rem(t + 1, half) < 2
    off_edge = (lax.rem(t + 1, half) // 2 + half // 2 - 1) // (half // 2)
    near = jnp.logical_and(lax.rem(t + 2, half) < 4, jnp.logical_not(edge))
    inner = lax.rem(t + 2, half) >= 4
    high = t // half
    last = lax.rem(t, half) // (half // 2)

    z_out, z_out_face = lax.rem(z + high + (1 - high) * (nz - 1), nz), high
    z_over, z_over_face = lax.rem(z + (1 - high) + high * (nz - 1), nz), 1 - high
    t_in, t_in_face = lax.rem(t + (1 - last) + last * (nt - 1), nt), 3 - last
    t_over, t_over_face = lax.rem(t + last + (1 - last) * (nt - 1), nt), 2 + last
    own_edge = t + off_edge * (2 * last - 1)
    partner = lax.rem(own_edge + half, nt)
    partner_near = partner + 1 - 2 * last
    t_pass = lax.rem(own_edge + last + (1 - last) * (nt - 1) + half, nt)
    t_pass_near = t_pass - 1 + 2 * last

    load_links = pltpu.make_async_copy(links_hbm, links, load_sem.at[0])
    load_source = pltpu.make_async_copy(src, vecs.at[0], load_sem.at[1])
    load_source.start()
    load_links.start()

    barrier = pltpu.get_barrier_semaphore()

    def greet(target):
        pl.semaphore_signal(barrier, inc=1, device_id=target, device_id_type=MESH)

    greet((t, z_out))
    greet((t_in, z))
    greet((t, z_over))

    @pl.when(jnp.logical_not(inner))
    def _():
        greet((partner, z))
        greet((partner, z_out))
        greet((t_pass, z))

    @pl.when(edge)
    def _():
        greet((partner_near, z))
        greet((partner_near, z_out))
        greet((t_pass_near, z))
        pl.semaphore_wait(barrier, 9)

    @pl.when(near)
    def _():
        greet((t_over, z))
        pl.semaphore_wait(barrier, 7)

    @pl.when(inner)
    def _():
        greet((t_over, z))
        pl.semaphore_wait(barrier, 4)

    def remote(block, slot, send, recv, target):
        return pltpu.make_async_remote_copy(
            src_ref=block, dst_ref=slot, send_sem=send, recv_sem=recv, device_id=target, device_id_type=MESH
        )

    def part(c):
        return pl.ds(c * CHUNK, CHUNK)

    def push(block, k, c, face, target):
        remote(block, faces.at[k, face, part(c)], send_sem.at[k, face], recv_sem.at[k, face, c], target).start()

    def issue_relay(block, k, c):
        @pl.when(edge)
        def _():
            remote(
                block,
                relayed.at[k, part(c)],
                send_sem.at[k, z_over_face],
                relay_sem.at[k, c],
                (partner + lax.rem(c, 2) * (partner_near - partner), z),
            ).start()

    def issue_edge(block, k, c):
        @pl.when(edge)
        def _():
            push(block, k, c, z_out_face, (t, z_out))
            push(block, k, c, t_in_face, (t_in, z))

    def push_all(block, k, c):
        push(block, k, c, z_out_face, (t, z_out))
        push(block, k, c, z_over_face, (t, z_over))
        push(block, k, c, t_over_face, (t_over, z))
        push(block, k, c, t_in_face, (t_in, z))

    def issue_near(block, k, c):
        @pl.when(near)
        def _():
            push_all(block, k, c)

    def issue_inner(block, k, c):
        @pl.when(inner)
        def _():
            push_all(block, k, c)

    def passed(k, c):
        block = relayed.at[k, part(c)]
        on_z = remote(
            block, faces.at[k, z_out_face, part(c)], pass_sem.at[k, 0], recv_sem.at[k, z_out_face, c], (partner, z_out)
        )
        on_t = remote(
            block, faces.at[k, t_over_face, part(c)], pass_sem.at[k, 1], recv_sem.at[k, t_over_face, c], (t_pass, z)
        )
        return on_z, on_t

    def issue_pass(k, c):
        odd = lax.rem(c, 2) == 1

        @pl.when(jnp.logical_or(jnp.logical_and(edge, jnp.logical_not(odd)), jnp.logical_and(near, odd)))
        def _():
            remote(
                vecs.at[k, part(c)], relayed.at[k, part(c)], send_sem.at[k, 0], relay_sem.at[k, c], (partner, z)
            ).wait_recv()
            on_z, on_t = passed(k, c)
            on_z.start()
            on_t.start()

    def arrived(k, c):
        for face in range(FACES):
            remote(
                vecs.at[k, part(c)], faces.at[k, face, part(c)], send_sem.at[k, face], recv_sem.at[k, face, c], (t_in, z)
            ).wait_recv()

    def at_home(k, s):
        row, x = s // NX, lax.rem(s, NX)
        here = [
            s,
            row * NX + lax.rem(x + 1, NX),
            row * NX + lax.rem(x + NX - 1, NX),
            lax.rem(s + NX, NYX),
            lax.rem(s + NX, NYX),
        ]
        total = jnp.zeros((DOF, RHS), jnp.float32)
        for d, at in enumerate(here):
            total += jnp.dot(links[s, d], vecs[k, at], preferred_element_type=jnp.float32)
        return total

    def applied(k, c, store_site):
        sites = [c * CHUNK + i for i in range(CHUNK)]
        totals = [at_home(k, s) for s in sites]
        arrived(k, c)
        for s, total in zip(sites, totals):
            for face in range(FACES):
                total += jnp.dot(links[s, 5 + face], faces[k, face, s], preferred_element_type=jnp.float32)
            store_site(s, total)

    def whose(step):
        return step // CHUNKS, lax.rem(step, CHUNKS)

    def send(issue, step):
        k, c = whose(step)
        issue(vecs.at[k, part(c)], k, c)

    windows = [
        (issue_inner, DIRECT),
        (issue_near, DIRECT_NEAR),
        (issue_edge, DIRECT_EDGE),
    ]

    for c in range(CHUNKS):
        issue_relay(src.at[part(c)], 0, jnp.int32(c))
        for issue, ahead in windows:
            if c < ahead:
                issue(src.at[part(c)], 0, c)
        if c >= CHUNKS - PASS:
            issue_pass(0, jnp.int32(c - (CHUNKS - PASS)))
    load_source.wait()
    load_links.wait()

    @pl.loop(0, STEPS - CHUNKS)
    def _(step):
        k, c = whose(step)

        def keep(s, total):
            vecs[k + 1, s] = total.astype(jnp.bfloat16)

        applied(k, c, keep)
        for issue, ahead in windows:
            send(issue, step + ahead)
        send(issue_relay, step + RELAY)
        issue_pass(*whose(step + PASS))

    def sent(k, sem, sites=NYX):
        block = pl.ds(0, sites)
        remote(vecs.at[k, block], faces.at[k, 0, block], sem, recv_sem.at[k, 0, 0], (t_in, z)).wait_send()

    def sent_round(k):
        sent(k, send_sem.at[k, z_out_face])
        sent(k, send_sem.at[k, z_over_face])
        sent(k, send_sem.at[k, t_in_face])

        @pl.when(jnp.logical_not(inner))
        def _():
            sent(k, pass_sem.at[k, 0], NYX // 2)
            sent(k, pass_sem.at[k, 1], NYX // 2)

        @pl.when(jnp.logical_not(edge))
        def _():
            sent(k, send_sem.at[k, t_over_face])

    for k in range(APPLIES - 2):
        sent_round(k)

    def store(c):
        return pltpu.make_async_copy(summed.at[part(c)], out.at[part(c)], out_sem.at[c])

    @pl.loop(0, CHUNKS)
    def _(c):
        def keep(s, total):
            summed[s] = total

        applied(APPLIES - 1, c, keep)
        store(c).start()

        for issue, ahead in windows:

            @pl.when(c + ahead < CHUNKS)
            def _():
                send(issue, STEPS - CHUNKS + c + ahead)

        @pl.when(c + PASS < CHUNKS)
        def _():
            issue_pass(APPLIES - 1, c + PASS)


    sent_round(APPLIES - 2)
    sent_round(APPLIES - 1)
    for c in range(CHUNKS):
        store(c).wait()


def shards(source, link_blocks):
    src = pltpu.with_memory_space_constraint(source.reshape(NYX, DOF, RHS), pltpu.HBM)
    links = pltpu.with_memory_space_constraint(link_blocks.reshape(NYX, DIRS, DOF, DOF), pltpu.HBM)
    total = pl.pallas_call(
        kernel,
        out_shape=jax.ShapeDtypeStruct((NYX, DOF, RHS), jnp.float32),
        in_specs=[pl.BlockSpec(memory_space=pl.ANY)] * 2,
        out_specs=pl.BlockSpec(memory_space=pl.ANY),
        scratch_shapes=[
            pltpu.VMEM((NYX, DIRS, DOF, DOF), jnp.bfloat16),
            pltpu.VMEM((APPLIES, NYX, DOF, RHS), jnp.bfloat16),
            pltpu.VMEM((APPLIES, FACES, NYX, DOF, RHS), jnp.bfloat16),
            pltpu.VMEM((APPLIES, NYX, DOF, RHS), jnp.bfloat16),
            pltpu.VMEM((NYX, DOF, RHS), jnp.float32),
            pltpu.SemaphoreType.DMA((2,)),
            pltpu.SemaphoreType.DMA((APPLIES, FACES)),
            pltpu.SemaphoreType.DMA((APPLIES, FACES, CHUNKS)),
            pltpu.SemaphoreType.DMA((APPLIES, CHUNKS)),
            pltpu.SemaphoreType.DMA((APPLIES, 2)),
            pltpu.SemaphoreType.DMA((CHUNKS,)),
        ],
        compiler_params=pltpu.CompilerParams(
            collective_id=0, has_side_effects=True, vmem_limit_bytes=40 * 2**20
        ),
        cost_estimate=pl.CostEstimate(
            flops=2 * APPLIES * NYX * DIRS * DOF * DOF * RHS, bytes_accessed=6 * 2**20, transcendentals=0
        ),
    )(src, links)
    return total.reshape(1, 1, NYX, DOF, RHS)


def solution(mesh):
    placed = (P("ta", "gz", None, None, None), P("ta", "gz", None, None, None, None))
    return jax.shard_map(
        shards,
        mesh=mesh,
        in_specs=placed,
        out_specs=P("ta", "gz", None, None, None),
        check_vma=False,
    )
```

```python
import jax
import jax.numpy as jnp
from jax import lax
from jax.experimental import pallas as pl
from jax.experimental.pallas import tpu as pltpu
from jax.sharding import PartitionSpec as P

DOF = 96
DIRS = 9
RHS = 128
NX = 8
NY = 2
NYX = NX * NY
APPLIES = 4
CHUNK = 2
CHUNKS = NYX // CHUNK
STEPS = APPLIES * CHUNKS
DIRECT_EDGE = 3
DIRECT_EDGE_IN = 7
DIRECT_NEAR = CHUNKS
DIRECT = CHUNKS
RELAY = CHUNKS
PASS = 3

FACES = 4
MESH = pl.DeviceIdType.MESH


def kernel(src, links_hbm, out, links, vecs, faces, relayed, summed, load_sem, send_sem, recv_sem, relay_sem, pass_sem, out_sem):
    t, z = lax.axis_index("ta"), lax.axis_index("gz")
    nt, nz = lax.axis_size("ta"), lax.axis_size("gz")
    half = nt // 2
    edge = lax.rem(t + 1, half) < 2
    off_edge = (lax.rem(t + 1, half) // 2 + half // 2 - 1) // (half // 2)
    near = jnp.logical_and(lax.rem(t + 2, half) < 4, jnp.logical_not(edge))
    inner = lax.rem(t + 2, half) >= 4
    high = t // half
    last = lax.rem(t, half) // (half // 2)

    z_out, z_out_face = lax.rem(z + high + (1 - high) * (nz - 1), nz), high
    z_over, z_over_face = lax.rem(z + (1 - high) + high * (nz - 1), nz), 1 - high
    t_in, t_in_face = lax.rem(t + (1 - last) + last * (nt - 1), nt), 3 - last
    t_over, t_over_face = lax.rem(t + last + (1 - last) * (nt - 1), nt), 2 + last
    own_edge = t + off_edge * (2 * last - 1)
    partner = lax.rem(own_edge + half, nt)
    partner_near = partner + 1 - 2 * last
    t_pass = lax.rem(own_edge + last + (1 - last) * (nt - 1) + half, nt)
    t_pass_near = t_pass - 1 + 2 * last

    load_links = pltpu.make_async_copy(links_hbm, links, load_sem.at[0])
    load_source = pltpu.make_async_copy(src, vecs.at[0], load_sem.at[1])
    load_source.start()
    load_links.start()

    barrier = pltpu.get_barrier_semaphore()

    def greet(target):
        pl.semaphore_signal(barrier, inc=1, device_id=target, device_id_type=MESH)

    greet((t, z_out))
    greet((t_in, z))
    greet((t, z_over))

    @pl.when(jnp.logical_not(inner))
    def _():
        greet((partner, z))
        greet((partner, z_out))
        greet((t_pass, z))

    @pl.when(edge)
    def _():
        greet((partner_near, z))
        greet((partner_near, z_out))
        greet((t_pass_near, z))
        pl.semaphore_wait(barrier, 9)

    @pl.when(near)
    def _():
        greet((t_over, z))
        pl.semaphore_wait(barrier, 7)

    @pl.when(inner)
    def _():
        greet((t_over, z))
        pl.semaphore_wait(barrier, 4)

    def remote(block, slot, send, recv, target):
        return pltpu.make_async_remote_copy(
            src_ref=block, dst_ref=slot, send_sem=send, recv_sem=recv, device_id=target, device_id_type=MESH
        )

    def part(c):
        return pl.ds(c * CHUNK, CHUNK)

    def push(block, k, c, face, target):
        remote(block, faces.at[k, face, part(c)], send_sem.at[k, face], recv_sem.at[k, face, c], target).start()

    def issue_relay(block, k, c):
        @pl.when(edge)
        def _():
            remote(
                block,
                relayed.at[k, part(c)],
                send_sem.at[k, z_over_face],
                relay_sem.at[k, c],
                (partner + lax.rem(c, 2) * (partner_near - partner), z),
            ).start()

    def issue_edge(block, k, c):
        @pl.when(edge)
        def _():
            push(block, k, c, z_out_face, (t, z_out))

    def issue_edge_in(block, k, c):
        @pl.when(edge)
        def _():
            push(block, k, c, t_in_face, (t_in, z))

    def push_all(block, k, c):
        push(block, k, c, z_out_face, (t, z_out))
        push(block, k, c, z_over_face, (t, z_over))
        push(block, k, c, t_over_face, (t_over, z))
        push(block, k, c, t_in_face, (t_in, z))

    def issue_near(block, k, c):
        @pl.when(near)
        def _():
            push_all(block, k, c)

    def issue_inner(block, k, c):
        @pl.when(inner)
        def _():
            push_all(block, k, c)

    def passed(k, c):
        block = relayed.at[k, part(c)]
        on_z = remote(
            block, faces.at[k, z_out_face, part(c)], pass_sem.at[k, 0], recv_sem.at[k, z_out_face, c], (partner, z_out)
        )
        on_t = remote(
            block, faces.at[k, t_over_face, part(c)], pass_sem.at[k, 1], recv_sem.at[k, t_over_face, c], (t_pass, z)
        )
        return on_z, on_t

    def issue_pass(k, c):
        odd = lax.rem(c, 2) == 1

        @pl.when(jnp.logical_or(jnp.logical_and(edge, jnp.logical_not(odd)), jnp.logical_and(near, odd)))
        def _():
            remote(
                vecs.at[k, part(c)], relayed.at[k, part(c)], send_sem.at[k, 0], relay_sem.at[k, c], (partner, z)
            ).wait_recv()
            on_z, on_t = passed(k, c)
            on_z.start()
            on_t.start()

    def arrived(k, c):
        for face in range(FACES):
            remote(
                vecs.at[k, part(c)], faces.at[k, face, part(c)], send_sem.at[k, face], recv_sem.at[k, face, c], (t_in, z)
            ).wait_recv()

    def at_home(k, s):
        row, x = s // NX, lax.rem(s, NX)
        here = [
            s,
            row * NX + lax.rem(x + 1, NX),
            row * NX + lax.rem(x + NX - 1, NX),
            lax.rem(s + NX, NYX),
            lax.rem(s + NX, NYX),
        ]
        total = jnp.zeros((DOF, RHS), jnp.float32)
        for d, at in enumerate(here):
            total += jnp.dot(links[s, d], vecs[k, at], preferred_element_type=jnp.float32)
        return total

    def applied(k, c, store_site):
        sites = [c * CHUNK + i for i in range(CHUNK)]
        totals = [at_home(k, s) for s in sites]
        arrived(k, c)
        for s, total in zip(sites, totals):
            for face in range(FACES):
                total += jnp.dot(links[s, 5 + face], faces[k, face, s], preferred_element_type=jnp.float32)
            store_site(s, total)

    def whose(step):
        return step // CHUNKS, lax.rem(step, CHUNKS)

    def send(issue, step):
        k, c = whose(step)
        issue(vecs.at[k, part(c)], k, c)

    windows = [
        (issue_inner, DIRECT),
        (issue_near, DIRECT_NEAR),
        (issue_edge, DIRECT_EDGE),
        (issue_edge_in, DIRECT_EDGE_IN),
    ]

    for c in range(CHUNKS):
        issue_relay(src.at[part(c)], 0, jnp.int32(c))
        for issue, ahead in windows:
            if c < ahead:
                issue(src.at[part(c)], 0, c)
        if c >= CHUNKS - PASS:
            issue_pass(0, jnp.int32(c - (CHUNKS - PASS)))
    load_source.wait()
    load_links.wait()

    @pl.loop(0, STEPS - CHUNKS)
    def _(step):
        k, c = whose(step)

        def keep(s, total):
            vecs[k + 1, s] = total.astype(jnp.bfloat16)

        applied(k, c, keep)
        for issue, ahead in windows:
            send(issue, step + ahead)
        send(issue_relay, step + RELAY)
        issue_pass(*whose(step + PASS))

    def sent(k, sem, sites=NYX):
        block = pl.ds(0, sites)
        remote(vecs.at[k, block], faces.at[k, 0, block], sem, recv_sem.at[k, 0, 0], (t_in, z)).wait_send()

    def sent_round(k):
        sent(k, send_sem.at[k, z_out_face])
        sent(k, send_sem.at[k, z_over_face])
        sent(k, send_sem.at[k, t_in_face])

        @pl.when(jnp.logical_not(inner))
        def _():
            sent(k, pass_sem.at[k, 0], NYX // 2)
            sent(k, pass_sem.at[k, 1], NYX // 2)

        @pl.when(jnp.logical_not(edge))
        def _():
            sent(k, send_sem.at[k, t_over_face])

    for k in range(APPLIES - 2):
        sent_round(k)

    def store(c):
        return pltpu.make_async_copy(summed.at[part(c)], out.at[part(c)], out_sem.at[c])

    @pl.loop(0, CHUNKS)
    def _(c):
        def keep(s, total):
            summed[s] = total

        applied(APPLIES - 1, c, keep)
        store(c).start()

        for issue, ahead in windows:

            @pl.when(c + ahead < CHUNKS)
            def _():
                send(issue, STEPS - CHUNKS + c + ahead)

        @pl.when(c + PASS < CHUNKS)
        def _():
            issue_pass(APPLIES - 1, c + PASS)


    sent_round(APPLIES - 2)
    sent_round(APPLIES - 1)
    for c in range(CHUNKS):
        store(c).wait()


def shards(source, link_blocks):
    src = pltpu.with_memory_space_constraint(source.reshape(NYX, DOF, RHS), pltpu.HBM)
    links = pltpu.with_memory_space_constraint(link_blocks.reshape(NYX, DIRS, DOF, DOF), pltpu.HBM)
    total = pl.pallas_call(
        kernel,
        out_shape=jax.ShapeDtypeStruct((NYX, DOF, RHS), jnp.float32),
        in_specs=[pl.BlockSpec(memory_space=pl.ANY)] * 2,
        out_specs=pl.BlockSpec(memory_space=pl.ANY),
        scratch_shapes=[
            pltpu.VMEM((NYX, DIRS, DOF, DOF), jnp.bfloat16),
            pltpu.VMEM((APPLIES, NYX, DOF, RHS), jnp.bfloat16),
            pltpu.VMEM((APPLIES, FACES, NYX, DOF, RHS), jnp.bfloat16),
            pltpu.VMEM((APPLIES, NYX, DOF, RHS), jnp.bfloat16),
            pltpu.VMEM((NYX, DOF, RHS), jnp.float32),
            pltpu.SemaphoreType.DMA((2,)),
            pltpu.SemaphoreType.DMA((APPLIES, FACES)),
            pltpu.SemaphoreType.DMA((APPLIES, FACES, CHUNKS)),
            pltpu.SemaphoreType.DMA((APPLIES, CHUNKS)),
            pltpu.SemaphoreType.DMA((APPLIES, 2)),
            pltpu.SemaphoreType.DMA((CHUNKS,)),
        ],
        compiler_params=pltpu.CompilerParams(
            collective_id=0, has_side_effects=True, vmem_limit_bytes=40 * 2**20
        ),
        cost_estimate=pl.CostEstimate(
            flops=2 * APPLIES * NYX * DIRS * DOF * DOF * RHS, bytes_accessed=6 * 2**20, transcendentals=0
        ),
    )(src, links)
    return total.reshape(1, 1, NYX, DOF, RHS)


def solution(mesh):
    placed = (P("ta", "gz", None, None, None), P("ta", "gz", None, None, None, None))
    return jax.shard_map(
        shards,
        mesh=mesh,
        in_specs=placed,
        out_specs=P("ta", "gz", None, None, None),
        check_vma=False,
    )
```

```python
import jax
import jax.numpy as jnp
from jax import lax
from jax.experimental import pallas as pl
from jax.experimental.pallas import tpu as pltpu
from jax.sharding import PartitionSpec as P

DOF = 96
DIRS = 9
RHS = 128
NX = 8
NY = 2
NYX = NX * NY
APPLIES = 4
CHUNK = 2
CHUNKS = NYX // CHUNK
STEPS = APPLIES * CHUNKS
DIRECT_EDGE = 6
DIRECT_NEAR = 7
DIRECT = 7
RELAY = CHUNKS
PASS = 5

FACES = 4
HOME = DIRS - FACES
MESH = pl.DeviceIdType.MESH


def kernel(src, links_hbm, out, links, home_links, face_links, vecs, faces, relayed, summed, load_sem, send_sem, recv_sem, relay_sem, pass_sem, out_sem):
    t, z = lax.axis_index("ta"), lax.axis_index("gz")
    nt, nz = lax.axis_size("ta"), lax.axis_size("gz")
    half = nt // 2
    edge = lax.rem(t + 1, half) < 2
    off_edge = (lax.rem(t + 1, half) // 2 + half // 2 - 1) // (half // 2)
    near = jnp.logical_and(lax.rem(t + 2, half) < 4, jnp.logical_not(edge))
    inner = lax.rem(t + 2, half) >= 4
    high = t // half
    last = lax.rem(t, half) // (half // 2)

    z_out, z_out_face = lax.rem(z + high + (1 - high) * (nz - 1), nz), high
    z_over, z_over_face = lax.rem(z + (1 - high) + high * (nz - 1), nz), 1 - high
    t_in, t_in_face = lax.rem(t + (1 - last) + last * (nt - 1), nt), 3 - last
    t_over, t_over_face = lax.rem(t + last + (1 - last) * (nt - 1), nt), 2 + last
    own_edge = t + off_edge * (2 * last - 1)
    partner = lax.rem(own_edge + half, nt)
    partner_near = partner + 1 - 2 * last
    t_pass = lax.rem(own_edge + last + (1 - last) * (nt - 1) + half, nt)
    t_pass_near = t_pass - 1 + 2 * last

    load_links = pltpu.make_async_copy(links_hbm, links, load_sem.at[0])
    load_source = pltpu.make_async_copy(src, vecs.at[0], load_sem.at[1])
    load_source.start()
    load_links.start()

    barrier = pltpu.get_barrier_semaphore()

    def greet(target):
        pl.semaphore_signal(barrier, inc=1, device_id=target, device_id_type=MESH)

    greet((t, z_out))
    greet((t_in, z))
    greet((t, z_over))

    @pl.when(jnp.logical_not(inner))
    def _():
        greet((partner, z))
        greet((partner, z_out))
        greet((t_pass, z))

    @pl.when(edge)
    def _():
        greet((partner_near, z))
        greet((partner_near, z_out))
        greet((t_pass_near, z))
        pl.semaphore_wait(barrier, 9)

    @pl.when(near)
    def _():
        greet((t_over, z))
        pl.semaphore_wait(barrier, 7)

    @pl.when(inner)
    def _():
        greet((t_over, z))
        pl.semaphore_wait(barrier, 4)

    def remote(block, slot, send, recv, target):
        return pltpu.make_async_remote_copy(
            src_ref=block, dst_ref=slot, send_sem=send, recv_sem=recv, device_id=target, device_id_type=MESH
        )

    def part(c):
        return pl.ds(c * CHUNK, CHUNK)

    def push(block, k, c, face, target):
        remote(block, faces.at[k, face, part(c)], send_sem.at[k, face], recv_sem.at[k, face, c], target).start()

    def issue_relay(block, k, c):
        @pl.when(edge)
        def _():
            remote(
                block,
                relayed.at[k, part(c)],
                send_sem.at[k, z_over_face],
                relay_sem.at[k, c],
                (partner + lax.rem(c, 2) * (partner_near - partner), z),
            ).start()

    def issue_edge(block, k, c):
        @pl.when(edge)
        def _():
            push(block, k, c, z_out_face, (t, z_out))
            push(block, k, c, t_in_face, (t_in, z))

    def push_all(block, k, c):
        push(block, k, c, z_out_face, (t, z_out))
        push(block, k, c, z_over_face, (t, z_over))
        push(block, k, c, t_over_face, (t_over, z))
        push(block, k, c, t_in_face, (t_in, z))

    def issue_near(block, k, c):
        @pl.when(near)
        def _():
            push_all(block, k, c)

    def issue_inner(block, k, c):
        @pl.when(inner)
        def _():
            push_all(block, k, c)

    def passed(k, c):
        block = relayed.at[k, part(c)]
        on_z = remote(
            block, faces.at[k, z_out_face, part(c)], pass_sem.at[k, 0], recv_sem.at[k, z_out_face, c], (partner, z_out)
        )
        on_t = remote(
            block, faces.at[k, t_over_face, part(c)], pass_sem.at[k, 1], recv_sem.at[k, t_over_face, c], (t_pass, z)
        )
        return on_z, on_t

    def issue_pass(k, c):
        odd = lax.rem(c, 2) == 1

        @pl.when(jnp.logical_or(jnp.logical_and(edge, jnp.logical_not(odd)), jnp.logical_and(near, odd)))
        def _():
            remote(
                vecs.at[k, part(c)], relayed.at[k, part(c)], send_sem.at[k, 0], relay_sem.at[k, c], (partner, z)
            ).wait_recv()
            on_z, on_t = passed(k, c)
            on_z.start()
            on_t.start()

    def arrived(k, c):
        for face in range(FACES):
            remote(
                vecs.at[k, part(c)], faces.at[k, face, part(c)], send_sem.at[k, face], recv_sem.at[k, face, c], (t_in, z)
            ).wait_recv()

    def at_home(k, s):
        row, x = s // NX, lax.rem(s, NX)
        here = [
            s,
            row * NX + lax.rem(x + 1, NX),
            row * NX + lax.rem(x + NX - 1, NX),
            lax.rem(s + NX, NYX),
            lax.rem(s + NX, NYX),
        ]
        stacked = jnp.concatenate([vecs[k, at] for at in here], axis=0)
        return jnp.dot(home_links[s], stacked, preferred_element_type=jnp.float32)

    def applied(k, c, store_site):
        sites = [c * CHUNK + i for i in range(CHUNK)]
        totals = [at_home(k, s) for s in sites]
        arrived(k, c)
        for s, total in zip(sites, totals):
            stacked = jnp.concatenate([faces[k, face, s] for face in range(FACES)], axis=0)
            total += jnp.dot(face_links[s], stacked, preferred_element_type=jnp.float32)
            store_site(s, total)

    def whose(step):
        return step // CHUNKS, lax.rem(step, CHUNKS)

    def send(issue, step):
        k, c = whose(step)
        issue(vecs.at[k, part(c)], k, c)

    windows = [
        (issue_inner, DIRECT),
        (issue_near, DIRECT_NEAR),
        (issue_edge, DIRECT_EDGE),
    ]

    for c in range(CHUNKS):
        issue_relay(src.at[part(c)], 0, jnp.int32(c))
        for issue, ahead in windows:
            if c < ahead:
                issue(src.at[part(c)], 0, c)
        if c >= CHUNKS - PASS:
            issue_pass(0, jnp.int32(c - (CHUNKS - PASS)))
    load_source.wait()
    load_links.wait()

    @pl.loop(0, NYX)
    def _(s):
        home_links[s] = jnp.concatenate([links[s, d] for d in range(HOME)], axis=1)
        face_links[s] = jnp.concatenate([links[s, HOME + face] for face in range(FACES)], axis=1)

    @pl.loop(0, STEPS - CHUNKS)
    def _(step):
        k, c = whose(step)

        def keep(s, total):
            vecs[k + 1, s] = total.astype(jnp.bfloat16)

        applied(k, c, keep)
        for issue, ahead in windows:
            send(issue, step + ahead)
        send(issue_relay, step + RELAY)
        issue_pass(*whose(step + PASS))

    def sent(k, sem, sites=NYX):
        block = pl.ds(0, sites)
        remote(vecs.at[k, block], faces.at[k, 0, block], sem, recv_sem.at[k, 0, 0], (t_in, z)).wait_send()

    def sent_round(k):
        sent(k, send_sem.at[k, z_out_face])
        sent(k, send_sem.at[k, z_over_face])
        sent(k, send_sem.at[k, t_in_face])

        @pl.when(jnp.logical_not(inner))
        def _():
            sent(k, pass_sem.at[k, 0], NYX // 2)
            sent(k, pass_sem.at[k, 1], NYX // 2)

        @pl.when(jnp.logical_not(edge))
        def _():
            sent(k, send_sem.at[k, t_over_face])

    for k in range(APPLIES - 2):
        sent_round(k)

    def store(c):
        return pltpu.make_async_copy(summed.at[part(c)], out.at[part(c)], out_sem.at[c])

    @pl.loop(0, CHUNKS)
    def _(c):
        def keep(s, total):
            summed[s] = total

        applied(APPLIES - 1, c, keep)
        store(c).start()

        for issue, ahead in windows:

            @pl.when(c + ahead < CHUNKS)
            def _():
                send(issue, STEPS - CHUNKS + c + ahead)

        @pl.when(c + PASS < CHUNKS)
        def _():
            issue_pass(APPLIES - 1, c + PASS)


    sent_round(APPLIES - 2)
    sent_round(APPLIES - 1)
    for c in range(CHUNKS):
        store(c).wait()


def shards(source, link_blocks):
    src = pltpu.with_memory_space_constraint(source.reshape(NYX, DOF, RHS), pltpu.HBM)
    links = pltpu.with_memory_space_constraint(link_blocks.reshape(NYX, DIRS, DOF, DOF), pltpu.HBM)
    total = pl.pallas_call(
        kernel,
        out_shape=jax.ShapeDtypeStruct((NYX, DOF, RHS), jnp.float32),
        in_specs=[pl.BlockSpec(memory_space=pl.ANY)] * 2,
        out_specs=pl.BlockSpec(memory_space=pl.ANY),
        scratch_shapes=[
            pltpu.VMEM((NYX, DIRS, DOF, DOF), jnp.bfloat16),
            pltpu.VMEM((NYX, DOF, HOME * DOF), jnp.bfloat16),
            pltpu.VMEM((NYX, DOF, FACES * DOF), jnp.bfloat16),
            pltpu.VMEM((APPLIES, NYX, DOF, RHS), jnp.bfloat16),
            pltpu.VMEM((APPLIES, FACES, NYX, DOF, RHS), jnp.bfloat16),
            pltpu.VMEM((APPLIES, NYX, DOF, RHS), jnp.bfloat16),
            pltpu.VMEM((NYX, DOF, RHS), jnp.float32),
            pltpu.SemaphoreType.DMA((2,)),
            pltpu.SemaphoreType.DMA((APPLIES, FACES)),
            pltpu.SemaphoreType.DMA((APPLIES, FACES, CHUNKS)),
            pltpu.SemaphoreType.DMA((APPLIES, CHUNKS)),
            pltpu.SemaphoreType.DMA((APPLIES, 2)),
            pltpu.SemaphoreType.DMA((CHUNKS,)),
        ],
        compiler_params=pltpu.CompilerParams(
            collective_id=0, has_side_effects=True, vmem_limit_bytes=40 * 2**20
        ),
        cost_estimate=pl.CostEstimate(
            flops=2 * APPLIES * NYX * DIRS * DOF * DOF * RHS, bytes_accessed=6 * 2**20, transcendentals=0
        ),
    )(src, links)
    return total.reshape(1, 1, NYX, DOF, RHS)


def solution(mesh):
    placed = (P("ta", "gz", None, None, None), P("ta", "gz", None, None, None, None))
    return jax.shard_map(
        shards,
        mesh=mesh,
        in_specs=placed,
        out_specs=P("ta", "gz", None, None, None),
        check_vma=False,
    )
```

```python
import jax
import jax.numpy as jnp
from jax import lax
from jax.experimental import pallas as pl
from jax.experimental.pallas import tpu as pltpu
from jax.sharding import PartitionSpec as P

DOF = 96
DIRS = 9
RHS = 128
NX = 8
NY = 2
NYX = NX * NY
APPLIES = 4
CHUNK = 2
CHUNKS = NYX // CHUNK
STEPS = APPLIES * CHUNKS
DIRECT_EDGE = 6
DIRECT_NEAR = 6
DIRECT = 6
RELAY = CHUNKS
PASS = 3

FACES = 4
MESH = pl.DeviceIdType.MESH


def kernel(src, links_hbm, out, links, vecs, faces, relayed, summed, load_sem, send_sem, recv_sem, relay_sem, pass_sem, out_sem):
    t, z = lax.axis_index("ta"), lax.axis_index("gz")
    nt, nz = lax.axis_size("ta"), lax.axis_size("gz")
    half = nt // 2
    edge = lax.rem(t + 1, half) < 2
    off_edge = (lax.rem(t + 1, half) // 2 + half // 2 - 1) // (half // 2)
    near = jnp.logical_and(lax.rem(t + 2, half) < 4, jnp.logical_not(edge))
    inner = lax.rem(t + 2, half) >= 4
    high = t // half
    last = lax.rem(t, half) // (half // 2)

    z_out, z_out_face = lax.rem(z + high + (1 - high) * (nz - 1), nz), high
    z_over, z_over_face = lax.rem(z + (1 - high) + high * (nz - 1), nz), 1 - high
    t_in, t_in_face = lax.rem(t + (1 - last) + last * (nt - 1), nt), 3 - last
    t_over, t_over_face = lax.rem(t + last + (1 - last) * (nt - 1), nt), 2 + last
    own_edge = t + off_edge * (2 * last - 1)
    partner = lax.rem(own_edge + half, nt)
    partner_near = partner + 1 - 2 * last
    t_pass = lax.rem(own_edge + last + (1 - last) * (nt - 1) + half, nt)
    t_pass_near = t_pass - 1 + 2 * last

    load_links = pltpu.make_async_copy(links_hbm, links, load_sem.at[0])
    load_source = pltpu.make_async_copy(src, vecs.at[0], load_sem.at[1])
    load_source.start()
    load_links.start()

    barrier = pltpu.get_barrier_semaphore()

    def greet(target):
        pl.semaphore_signal(barrier, inc=1, device_id=target, device_id_type=MESH)

    greet((t, z_out))
    greet((t_in, z))
    greet((t, z_over))

    @pl.when(jnp.logical_not(inner))
    def _():
        greet((partner, z))
        greet((partner, z_out))
        greet((t_pass, z))

    @pl.when(edge)
    def _():
        greet((partner_near, z))
        greet((partner_near, z_out))
        greet((t_pass_near, z))
        pl.semaphore_wait(barrier, 9)

    @pl.when(near)
    def _():
        greet((t_over, z))
        pl.semaphore_wait(barrier, 7)

    @pl.when(inner)
    def _():
        greet((t_over, z))
        pl.semaphore_wait(barrier, 4)

    def remote(block, slot, send, recv, target):
        return pltpu.make_async_remote_copy(
            src_ref=block, dst_ref=slot, send_sem=send, recv_sem=recv, device_id=target, device_id_type=MESH
        )

    def part(c):
        return pl.ds(c * CHUNK, CHUNK)

    def push(block, k, c, face, target):
        remote(block, faces.at[k, face, part(c)], send_sem.at[k, face], recv_sem.at[k, face, c], target).start()

    def issue_relay(block, k, c):
        @pl.when(edge)
        def _():
            remote(
                block,
                relayed.at[k, part(c)],
                send_sem.at[k, z_over_face],
                relay_sem.at[k, c],
                (partner + lax.rem(c, 2) * (partner_near - partner), z),
            ).start()

    def issue_edge(block, k, c):
        @pl.when(edge)
        def _():
            push(block, k, c, z_out_face, (t, z_out))
            push(block, k, c, t_in_face, (t_in, z))

    def push_all(block, k, c):
        push(block, k, c, z_out_face, (t, z_out))
        push(block, k, c, z_over_face, (t, z_over))
        push(block, k, c, t_over_face, (t_over, z))
        push(block, k, c, t_in_face, (t_in, z))

    def issue_near(block, k, c):
        @pl.when(near)
        def _():
            push_all(block, k, c)

    def issue_inner(block, k, c):
        @pl.when(inner)
        def _():
            push_all(block, k, c)

    def passed(k, c):
        block = relayed.at[k, part(c)]
        on_z = remote(
            block, faces.at[k, z_out_face, part(c)], pass_sem.at[k, 0], recv_sem.at[k, z_out_face, c], (partner, z_out)
        )
        on_t = remote(
            block, faces.at[k, t_over_face, part(c)], pass_sem.at[k, 1], recv_sem.at[k, t_over_face, c], (t_pass, z)
        )
        return on_z, on_t

    def issue_pass(k, c):
        odd = lax.rem(c, 2) == 1

        @pl.when(jnp.logical_or(jnp.logical_and(edge, jnp.logical_not(odd)), jnp.logical_and(near, odd)))
        def _():
            remote(
                vecs.at[k, part(c)], relayed.at[k, part(c)], send_sem.at[k, 0], relay_sem.at[k, c], (partner, z)
            ).wait_recv()
            on_z, on_t = passed(k, c)
            on_z.start()
            on_t.start()

    def arrived(k, c):
        for face in range(FACES):
            remote(
                vecs.at[k, part(c)], faces.at[k, face, part(c)], send_sem.at[k, face], recv_sem.at[k, face, c], (t_in, z)
            ).wait_recv()

    def at_home(k, s):
        row, x = s // NX, lax.rem(s, NX)
        here = [
            s,
            row * NX + lax.rem(x + 1, NX),
            row * NX + lax.rem(x + NX - 1, NX),
            lax.rem(s + NX, NYX),
            lax.rem(s + NX, NYX),
        ]
        total = jnp.zeros((DOF, RHS), jnp.float32)
        for d, at in enumerate(here):
            total += jnp.dot(links[s, d], vecs[k, at], preferred_element_type=jnp.float32)
        return total

    def applied(k, c, store_site):
        sites = [c * CHUNK + i for i in range(CHUNK)]
        totals = [at_home(k, s) for s in sites]
        arrived(k, c)
        for s, total in zip(sites, totals):
            for face in range(FACES):
                total += jnp.dot(links[s, 5 + face], faces[k, face, s], preferred_element_type=jnp.float32)
            store_site(s, total)

    def whose(step):
        return step // CHUNKS, lax.rem(step, CHUNKS)

    def send(issue, step):
        k, c = whose(step)
        issue(vecs.at[k, part(c)], k, c)

    windows = [
        (issue_inner, DIRECT),
        (issue_near, DIRECT_NEAR),
        (issue_edge, DIRECT_EDGE),
    ]

    for c in range(CHUNKS):
        issue_relay(src.at[part(c)], 0, jnp.int32(c))
        for issue, ahead in windows:
            if c < ahead:
                issue(src.at[part(c)], 0, c)
        if c >= CHUNKS - PASS:
            issue_pass(0, jnp.int32(c - (CHUNKS - PASS)))
    load_source.wait()
    load_links.wait()

    @pl.loop(0, STEPS - CHUNKS)
    def _(step):
        k, c = whose(step)

        def keep(s, total):
            vecs[k + 1, s] = total.astype(jnp.bfloat16)

        applied(k, c, keep)
        for issue, ahead in windows:
            send(issue, step + ahead)
        send(issue_relay, step + RELAY)
        issue_pass(*whose(step + PASS))

    def sent(k, sem, sites=NYX):
        block = pl.ds(0, sites)
        remote(vecs.at[k, block], faces.at[k, 0, block], sem, recv_sem.at[k, 0, 0], (t_in, z)).wait_send()

    def sent_round(k):
        sent(k, send_sem.at[k, z_out_face])
        sent(k, send_sem.at[k, z_over_face])
        sent(k, send_sem.at[k, t_in_face])

        @pl.when(jnp.logical_not(inner))
        def _():
            sent(k, pass_sem.at[k, 0], NYX // 2)
            sent(k, pass_sem.at[k, 1], NYX // 2)

        @pl.when(jnp.logical_not(edge))
        def _():
            sent(k, send_sem.at[k, t_over_face])

    for k in range(APPLIES - 2):
        sent_round(k)

    def store(c):
        return pltpu.make_async_copy(summed.at[part(c)], out.at[part(c)], out_sem.at[c])

    @pl.loop(0, CHUNKS)
    def _(c):
        def keep(s, total):
            summed[s] = total

        applied(APPLIES - 1, c, keep)
        store(c).start()

        for issue, ahead in windows:

            @pl.when(c + ahead < CHUNKS)
            def _():
                send(issue, STEPS - CHUNKS + c + ahead)

        @pl.when(c + PASS < CHUNKS)
        def _():
            issue_pass(APPLIES - 1, c + PASS)


    sent_round(APPLIES - 2)
    sent_round(APPLIES - 1)
    for c in range(CHUNKS):
        store(c).wait()


def shards(source, link_blocks):
    src = pltpu.with_memory_space_constraint(source.reshape(NYX, DOF, RHS), pltpu.HBM)
    links = pltpu.with_memory_space_constraint(link_blocks.reshape(NYX, DIRS, DOF, DOF), pltpu.HBM)
    total = pl.pallas_call(
        kernel,
        out_shape=jax.ShapeDtypeStruct((NYX, DOF, RHS), jnp.float32),
        in_specs=[pl.BlockSpec(memory_space=pl.ANY)] * 2,
        out_specs=pl.BlockSpec(memory_space=pl.ANY),
        scratch_shapes=[
            pltpu.VMEM((NYX, DIRS, DOF, DOF), jnp.bfloat16),
            pltpu.VMEM((APPLIES, NYX, DOF, RHS), jnp.bfloat16),
            pltpu.VMEM((APPLIES, FACES, NYX, DOF, RHS), jnp.bfloat16),
            pltpu.VMEM((APPLIES, NYX, DOF, RHS), jnp.bfloat16),
            pltpu.VMEM((NYX, DOF, RHS), jnp.float32),
            pltpu.SemaphoreType.DMA((2,)),
            pltpu.SemaphoreType.DMA((APPLIES, FACES)),
            pltpu.SemaphoreType.DMA((APPLIES, FACES, CHUNKS)),
            pltpu.SemaphoreType.DMA((APPLIES, CHUNKS)),
            pltpu.SemaphoreType.DMA((APPLIES, 2)),
            pltpu.SemaphoreType.DMA((CHUNKS,)),
        ],
        compiler_params=pltpu.CompilerParams(
            collective_id=0, has_side_effects=True, vmem_limit_bytes=40 * 2**20
        ),
        cost_estimate=pl.CostEstimate(
            flops=2 * APPLIES * NYX * DIRS * DOF * DOF * RHS, bytes_accessed=6 * 2**20, transcendentals=0
        ),
    )(src, links)
    return total.reshape(1, 1, NYX, DOF, RHS)


def solution(mesh):
    placed = (P("ta", "gz", None, None, None), P("ta", "gz", None, None, None, None))
    return jax.shard_map(
        shards,
        mesh=mesh,
        in_specs=placed,
        out_specs=P("ta", "gz", None, None, None),
        check_vma=False,
    )
```

```python
import jax
import jax.numpy as jnp
from jax import lax
from jax.experimental import pallas as pl
from jax.experimental.pallas import tpu as pltpu
from jax.sharding import PartitionSpec as P

DOF = 96
DIRS = 9
RHS = 128
NX = 8
NY = 2
NYX = NX * NY
APPLIES = 4
CHUNK = 2
CHUNKS = NYX // CHUNK
STEPS = APPLIES * CHUNKS
DIRECT_EDGE = 6
DIRECT_NEAR = 6
DIRECT = 6
RELAY = CHUNKS
PASS = 6

FACES = 4
MESH = pl.DeviceIdType.MESH


def kernel(src, links_hbm, out, links, vecs, faces, relayed, summed, load_sem, send_sem, recv_sem, relay_sem, pass_sem, out_sem):
    t, z = lax.axis_index("ta"), lax.axis_index("gz")
    nt, nz = lax.axis_size("ta"), lax.axis_size("gz")
    half = nt // 2
    edge = lax.rem(t + 1, half) < 2
    off_edge = (lax.rem(t + 1, half) // 2 + half // 2 - 1) // (half // 2)
    near = jnp.logical_and(lax.rem(t + 2, half) < 4, jnp.logical_not(edge))
    inner = lax.rem(t + 2, half) >= 4
    high = t // half
    last = lax.rem(t, half) // (half // 2)

    z_out, z_out_face = lax.rem(z + high + (1 - high) * (nz - 1), nz), high
    z_over, z_over_face = lax.rem(z + (1 - high) + high * (nz - 1), nz), 1 - high
    t_in, t_in_face = lax.rem(t + (1 - last) + last * (nt - 1), nt), 3 - last
    t_over, t_over_face = lax.rem(t + last + (1 - last) * (nt - 1), nt), 2 + last
    own_edge = t + off_edge * (2 * last - 1)
    partner = lax.rem(own_edge + half, nt)
    partner_near = partner + 1 - 2 * last
    t_pass = lax.rem(own_edge + last + (1 - last) * (nt - 1) + half, nt)
    t_pass_near = t_pass - 1 + 2 * last

    load_links = pltpu.make_async_copy(links_hbm, links, load_sem.at[0])
    load_source = pltpu.make_async_copy(src, vecs.at[0], load_sem.at[1])
    load_source.start()
    load_links.start()

    barrier = pltpu.get_barrier_semaphore()

    def greet(target):
        pl.semaphore_signal(barrier, inc=1, device_id=target, device_id_type=MESH)

    greet((t, z_out))
    greet((t_in, z))
    greet((t, z_over))

    @pl.when(jnp.logical_not(inner))
    def _():
        greet((partner, z))
        greet((partner, z_out))
        greet((t_pass, z))

    @pl.when(edge)
    def _():
        greet((partner_near, z))
        greet((partner_near, z_out))
        greet((t_pass_near, z))
        pl.semaphore_wait(barrier, 9)

    @pl.when(near)
    def _():
        greet((t_over, z))
        pl.semaphore_wait(barrier, 7)

    @pl.when(inner)
    def _():
        greet((t_over, z))
        pl.semaphore_wait(barrier, 4)

    def remote(block, slot, send, recv, target):
        return pltpu.make_async_remote_copy(
            src_ref=block, dst_ref=slot, send_sem=send, recv_sem=recv, device_id=target, device_id_type=MESH
        )

    def part(c):
        return pl.ds(c * CHUNK, CHUNK)

    def push(block, k, c, face, target):
        remote(block, faces.at[k, face, part(c)], send_sem.at[k, face], recv_sem.at[k, face, c], target).start()

    def issue_relay(block, k, c):
        @pl.when(edge)
        def _():
            remote(
                block,
                relayed.at[k, part(c)],
                send_sem.at[k, z_over_face],
                relay_sem.at[k, c],
                (partner + lax.rem(c, 2) * (partner_near - partner), z),
            ).start()

    def issue_edge(block, k, c):
        @pl.when(edge)
        def _():
            push(block, k, c, z_out_face, (t, z_out))
            push(block, k, c, t_in_face, (t_in, z))

    def push_all(block, k, c):
        push(block, k, c, z_out_face, (t, z_out))
        push(block, k, c, z_over_face, (t, z_over))
        push(block, k, c, t_over_face, (t_over, z))
        push(block, k, c, t_in_face, (t_in, z))

    def issue_near(block, k, c):
        @pl.when(near)
        def _():
            push_all(block, k, c)

    def issue_inner(block, k, c):
        @pl.when(inner)
        def _():
            push_all(block, k, c)

    def passed(k, c):
        block = relayed.at[k, part(c)]
        on_z = remote(
            block, faces.at[k, z_out_face, part(c)], pass_sem.at[k, 0], recv_sem.at[k, z_out_face, c], (partner, z_out)
        )
        on_t = remote(
            block, faces.at[k, t_over_face, part(c)], pass_sem.at[k, 1], recv_sem.at[k, t_over_face, c], (t_pass, z)
        )
        return on_z, on_t

    def issue_pass(k, c):
        odd = lax.rem(c, 2) == 1

        @pl.when(jnp.logical_or(jnp.logical_and(edge, jnp.logical_not(odd)), jnp.logical_and(near, odd)))
        def _():
            remote(
                vecs.at[k, part(c)], relayed.at[k, part(c)], send_sem.at[k, 0], relay_sem.at[k, c], (partner, z)
            ).wait_recv()
            on_z, on_t = passed(k, c)
            on_z.start()
            on_t.start()

    def arrived(k, c):
        for face in range(FACES):
            remote(
                vecs.at[k, part(c)], faces.at[k, face, part(c)], send_sem.at[k, face], recv_sem.at[k, face, c], (t_in, z)
            ).wait_recv()

    def at_home(k, s):
        row, x = s // NX, lax.rem(s, NX)
        here = [
            s,
            row * NX + lax.rem(x + 1, NX),
            row * NX + lax.rem(x + NX - 1, NX),
            lax.rem(s + NX, NYX),
            lax.rem(s + NX, NYX),
        ]
        total = jnp.zeros((DOF, RHS), jnp.float32)
        for d, at in enumerate(here):
            total += jnp.dot(links[s, d], vecs[k, at], preferred_element_type=jnp.float32)
        return total

    def applied(k, c, store_site):
        sites = [c * CHUNK + i for i in range(CHUNK)]
        totals = [at_home(k, s) for s in sites]
        arrived(k, c)
        for s, total in zip(sites, totals):
            for face in range(FACES):
                total += jnp.dot(links[s, 5 + face], faces[k, face, s], preferred_element_type=jnp.float32)
            store_site(s, total)

    def whose(step):
        return step // CHUNKS, lax.rem(step, CHUNKS)

    def send(issue, step):
        k, c = whose(step)
        issue(vecs.at[k, part(c)], k, c)

    windows = [
        (issue_inner, DIRECT),
        (issue_near, DIRECT_NEAR),
        (issue_edge, DIRECT_EDGE),
    ]

    for c in range(CHUNKS):
        issue_relay(src.at[part(c)], 0, jnp.int32(c))
        for issue, ahead in windows:
            if c < ahead:
                issue(src.at[part(c)], 0, c)
        if c >= CHUNKS - PASS:
            issue_pass(0, jnp.int32(c - (CHUNKS - PASS)))
    load_source.wait()
    load_links.wait()

    @pl.loop(0, STEPS - CHUNKS)
    def _(step):
        k, c = whose(step)

        def keep(s, total):
            vecs[k + 1, s] = total.astype(jnp.bfloat16)

        applied(k, c, keep)
        for issue, ahead in windows:
            send(issue, step + ahead)
        send(issue_relay, step + RELAY)
        issue_pass(*whose(step + PASS))

    def sent(k, sem, sites=NYX):
        block = pl.ds(0, sites)
        remote(vecs.at[k, block], faces.at[k, 0, block], sem, recv_sem.at[k, 0, 0], (t_in, z)).wait_send()

    def sent_round(k):
        sent(k, send_sem.at[k, z_out_face])
        sent(k, send_sem.at[k, z_over_face])
        sent(k, send_sem.at[k, t_in_face])

        @pl.when(jnp.logical_not(inner))
        def _():
            sent(k, pass_sem.at[k, 0], NYX // 2)
            sent(k, pass_sem.at[k, 1], NYX // 2)

        @pl.when(jnp.logical_not(edge))
        def _():
            sent(k, send_sem.at[k, t_over_face])

    for k in range(APPLIES - 2):
        sent_round(k)

    def store(c):
        return pltpu.make_async_copy(summed.at[part(c)], out.at[part(c)], out_sem.at[c])

    @pl.loop(0, CHUNKS)
    def _(c):
        def keep(s, total):
            summed[s] = total

        applied(APPLIES - 1, c, keep)
        store(c).start()

        for issue, ahead in windows:

            @pl.when(c + ahead < CHUNKS)
            def _():
                send(issue, STEPS - CHUNKS + c + ahead)

        @pl.when(c + PASS < CHUNKS)
        def _():
            issue_pass(APPLIES - 1, c + PASS)


    sent_round(APPLIES - 2)
    sent_round(APPLIES - 1)
    for c in range(CHUNKS):
        store(c).wait()


def shards(source, link_blocks):
    src = pltpu.with_memory_space_constraint(source.reshape(NYX, DOF, RHS), pltpu.HBM)
    links = pltpu.with_memory_space_constraint(link_blocks.reshape(NYX, DIRS, DOF, DOF), pltpu.HBM)
    total = pl.pallas_call(
        kernel,
        out_shape=jax.ShapeDtypeStruct((NYX, DOF, RHS), jnp.float32),
        in_specs=[pl.BlockSpec(memory_space=pl.ANY)] * 2,
        out_specs=pl.BlockSpec(memory_space=pl.ANY),
        scratch_shapes=[
            pltpu.VMEM((NYX, DIRS, DOF, DOF), jnp.bfloat16),
            pltpu.VMEM((APPLIES, NYX, DOF, RHS), jnp.bfloat16),
            pltpu.VMEM((APPLIES, FACES, NYX, DOF, RHS), jnp.bfloat16),
            pltpu.VMEM((APPLIES, NYX, DOF, RHS), jnp.bfloat16),
            pltpu.VMEM((NYX, DOF, RHS), jnp.float32),
            pltpu.SemaphoreType.DMA((2,)),
            pltpu.SemaphoreType.DMA((APPLIES, FACES)),
            pltpu.SemaphoreType.DMA((APPLIES, FACES, CHUNKS)),
            pltpu.SemaphoreType.DMA((APPLIES, CHUNKS)),
            pltpu.SemaphoreType.DMA((APPLIES, 2)),
            pltpu.SemaphoreType.DMA((CHUNKS,)),
        ],
        compiler_params=pltpu.CompilerParams(
            collective_id=0, has_side_effects=True, vmem_limit_bytes=40 * 2**20
        ),
        cost_estimate=pl.CostEstimate(
            flops=2 * APPLIES * NYX * DIRS * DOF * DOF * RHS, bytes_accessed=6 * 2**20, transcendentals=0
        ),
    )(src, links)
    return total.reshape(1, 1, NYX, DOF, RHS)


def solution(mesh):
    placed = (P("ta", "gz", None, None, None), P("ta", "gz", None, None, None, None))
    return jax.shard_map(
        shards,
        mesh=mesh,
        in_specs=placed,
        out_specs=P("ta", "gz", None, None, None),
        check_vma=False,
    )
```

```python
import jax
import jax.numpy as jnp
from jax import lax
from jax.experimental import pallas as pl
from jax.experimental.pallas import tpu as pltpu
from jax.sharding import PartitionSpec as P

DOF = 96
DIRS = 9
RHS = 128
NX = 8
NY = 2
NYX = NX * NY
APPLIES = 4
CHUNK = 2
CHUNKS = NYX // CHUNK
STEPS = APPLIES * CHUNKS
DIRECT_EDGE = 5
DIRECT_NEAR = 6
DIRECT = 6
RELAY = CHUNKS
PASS = 5

FACES = 4
MESH = pl.DeviceIdType.MESH


def kernel(src, links_hbm, out, links, vecs, faces, relayed, load_sem, send_sem, recv_sem, relay_sem, pass_sem):
    t, z = lax.axis_index("ta"), lax.axis_index("gz")
    nt, nz = lax.axis_size("ta"), lax.axis_size("gz")
    half = nt // 2
    edge = lax.rem(t + 1, half) < 2
    off_edge = (lax.rem(t + 1, half) // 2 + half // 2 - 1) // (half // 2)
    near = jnp.logical_and(lax.rem(t + 2, half) < 4, jnp.logical_not(edge))
    inner = lax.rem(t + 2, half) >= 4
    high = t // half
    last = lax.rem(t, half) // (half // 2)

    z_out, z_out_face = lax.rem(z + high + (1 - high) * (nz - 1), nz), high
    z_over, z_over_face = lax.rem(z + (1 - high) + high * (nz - 1), nz), 1 - high
    t_in, t_in_face = lax.rem(t + (1 - last) + last * (nt - 1), nt), 3 - last
    t_over, t_over_face = lax.rem(t + last + (1 - last) * (nt - 1), nt), 2 + last
    own_edge = t + off_edge * (2 * last - 1)
    partner = lax.rem(own_edge + half, nt)
    partner_near = partner + 1 - 2 * last
    t_pass = lax.rem(own_edge + last + (1 - last) * (nt - 1) + half, nt)
    t_pass_near = t_pass - 1 + 2 * last

    load_links = pltpu.make_async_copy(links_hbm, links, load_sem.at[0])
    load_source = pltpu.make_async_copy(src, vecs.at[0], load_sem.at[1])
    load_source.start()
    load_links.start()

    barrier = pltpu.get_barrier_semaphore()

    def greet(target):
        pl.semaphore_signal(barrier, inc=1, device_id=target, device_id_type=MESH)

    greet((t, z_out))
    greet((t_in, z))
    greet((t, z_over))

    @pl.when(jnp.logical_not(inner))
    def _():
        greet((partner, z))
        greet((partner, z_out))
        greet((t_pass, z))

    @pl.when(edge)
    def _():
        greet((partner_near, z))
        greet((partner_near, z_out))
        greet((t_pass_near, z))
        pl.semaphore_wait(barrier, 9)

    @pl.when(near)
    def _():
        greet((t_over, z))
        pl.semaphore_wait(barrier, 7)

    @pl.when(inner)
    def _():
        greet((t_over, z))
        pl.semaphore_wait(barrier, 4)

    def remote(block, slot, send, recv, target):
        return pltpu.make_async_remote_copy(
            src_ref=block, dst_ref=slot, send_sem=send, recv_sem=recv, device_id=target, device_id_type=MESH
        )

    def part(c):
        return pl.ds(c * CHUNK, CHUNK)

    def push(block, k, c, face, target):
        remote(block, faces.at[k, face, part(c)], send_sem.at[k, face], recv_sem.at[k, face, c], target).start()

    def issue_relay(block, k, c):
        @pl.when(edge)
        def _():
            remote(
                block,
                relayed.at[k, part(c)],
                send_sem.at[k, z_over_face],
                relay_sem.at[k, c],
                (partner + lax.rem(c, 2) * (partner_near - partner), z),
            ).start()

    def issue_edge(block, k, c):
        @pl.when(edge)
        def _():
            push(block, k, c, z_out_face, (t, z_out))
            push(block, k, c, t_in_face, (t_in, z))

    def push_all(block, k, c):
        push(block, k, c, z_out_face, (t, z_out))
        push(block, k, c, z_over_face, (t, z_over))
        push(block, k, c, t_over_face, (t_over, z))
        push(block, k, c, t_in_face, (t_in, z))

    def issue_near(block, k, c):
        @pl.when(near)
        def _():
            push_all(block, k, c)

    def issue_inner(block, k, c):
        @pl.when(inner)
        def _():
            push_all(block, k, c)

    def passed(k, c):
        block = relayed.at[k, part(c)]
        on_z = remote(
            block, faces.at[k, z_out_face, part(c)], pass_sem.at[k, 0], recv_sem.at[k, z_out_face, c], (partner, z_out)
        )
        on_t = remote(
            block, faces.at[k, t_over_face, part(c)], pass_sem.at[k, 1], recv_sem.at[k, t_over_face, c], (t_pass, z)
        )
        return on_z, on_t

    def issue_pass(k, c):
        odd = lax.rem(c, 2) == 1

        @pl.when(jnp.logical_or(jnp.logical_and(edge, jnp.logical_not(odd)), jnp.logical_and(near, odd)))
        def _():
            remote(
                vecs.at[k, part(c)], relayed.at[k, part(c)], send_sem.at[k, 0], relay_sem.at[k, c], (partner, z)
            ).wait_recv()
            on_z, on_t = passed(k, c)
            on_z.start()
            on_t.start()

    def arrived(k, c):
        for face in range(FACES):
            remote(
                vecs.at[k, part(c)], faces.at[k, face, part(c)], send_sem.at[k, face], recv_sem.at[k, face, c], (t_in, z)
            ).wait_recv()

    def at_home(k, s):
        row, x = s // NX, lax.rem(s, NX)
        here = [
            s,
            row * NX + lax.rem(x + 1, NX),
            row * NX + lax.rem(x + NX - 1, NX),
            lax.rem(s + NX, NYX),
            lax.rem(s + NX, NYX),
        ]
        total = jnp.zeros((DOF, RHS), jnp.float32)
        for d, at in enumerate(here):
            total += jnp.dot(links[s, d], vecs[k, at], preferred_element_type=jnp.float32)
        return total

    def applied(k, c, store_site):
        sites = [c * CHUNK + i for i in range(CHUNK)]
        totals = [at_home(k, s) for s in sites]
        arrived(k, c)
        for s, total in zip(sites, totals):
            for face in range(FACES):
                total += jnp.dot(links[s, 5 + face], faces[k, face, s], preferred_element_type=jnp.float32)
            store_site(s, total)

    def whose(step):
        return step // CHUNKS, lax.rem(step, CHUNKS)

    def send(issue, step):
        k, c = whose(step)
        issue(vecs.at[k, part(c)], k, c)

    windows = [
        (issue_inner, DIRECT),
        (issue_near, DIRECT_NEAR),
        (issue_edge, DIRECT_EDGE),
    ]

    for c in range(CHUNKS):
        issue_relay(src.at[part(c)], 0, jnp.int32(c))
        for issue, ahead in windows:
            if c < ahead:
                issue(src.at[part(c)], 0, c)
        if c >= CHUNKS - PASS:
            issue_pass(0, jnp.int32(c - (CHUNKS - PASS)))
    load_source.wait()
    load_links.wait()

    @pl.loop(0, STEPS - CHUNKS)
    def _(step):
        k, c = whose(step)

        def keep(s, total):
            vecs[k + 1, s] = total.astype(jnp.bfloat16)

        applied(k, c, keep)
        for issue, ahead in windows:
            send(issue, step + ahead)
        send(issue_relay, step + RELAY)
        issue_pass(*whose(step + PASS))

    def sent(k, sem, sites=NYX):
        block = pl.ds(0, sites)
        remote(vecs.at[k, block], faces.at[k, 0, block], sem, recv_sem.at[k, 0, 0], (t_in, z)).wait_send()

    def sent_round(k):
        sent(k, send_sem.at[k, z_out_face])
        sent(k, send_sem.at[k, z_over_face])
        sent(k, send_sem.at[k, t_in_face])

        @pl.when(jnp.logical_not(inner))
        def _():
            sent(k, pass_sem.at[k, 0], NYX // 2)
            sent(k, pass_sem.at[k, 1], NYX // 2)

        @pl.when(jnp.logical_not(edge))
        def _():
            sent(k, send_sem.at[k, t_over_face])

    for k in range(APPLIES - 2):
        sent_round(k)

    @pl.loop(0, CHUNKS)
    def _(c):
        def keep(s, total):
            out[s] = total

        applied(APPLIES - 1, c, keep)

        for issue, ahead in windows:

            @pl.when(c + ahead < CHUNKS)
            def _():
                send(issue, STEPS - CHUNKS + c + ahead)

        @pl.when(c + PASS < CHUNKS)
        def _():
            issue_pass(APPLIES - 1, c + PASS)


    sent_round(APPLIES - 2)
    sent_round(APPLIES - 1)


def shards(source, link_blocks):
    src = pltpu.with_memory_space_constraint(source.reshape(NYX, DOF, RHS), pltpu.HBM)
    links = pltpu.with_memory_space_constraint(link_blocks.reshape(NYX, DIRS, DOF, DOF), pltpu.HBM)
    total = pl.pallas_call(
        kernel,
        out_shape=pltpu.VMEM((NYX, DOF, RHS), jnp.float32),
        in_specs=[pl.BlockSpec(memory_space=pl.ANY)] * 2,
        out_specs=pl.BlockSpec(memory_space=pltpu.VMEM),
        scratch_shapes=[
            pltpu.VMEM((NYX, DIRS, DOF, DOF), jnp.bfloat16),
            pltpu.VMEM((APPLIES, NYX, DOF, RHS), jnp.bfloat16),
            pltpu.VMEM((APPLIES, FACES, NYX, DOF, RHS), jnp.bfloat16),
            pltpu.VMEM((APPLIES, NYX, DOF, RHS), jnp.bfloat16),
            pltpu.SemaphoreType.DMA((2,)),
            pltpu.SemaphoreType.DMA((APPLIES, FACES)),
            pltpu.SemaphoreType.DMA((APPLIES, FACES, CHUNKS)),
            pltpu.SemaphoreType.DMA((APPLIES, CHUNKS)),
            pltpu.SemaphoreType.DMA((APPLIES, 2)),
        ],
        compiler_params=pltpu.CompilerParams(
            collective_id=0, has_side_effects=True, vmem_limit_bytes=40 * 2**20
        ),
        cost_estimate=pl.CostEstimate(
            flops=2 * APPLIES * NYX * DIRS * DOF * DOF * RHS, bytes_accessed=6 * 2**20, transcendentals=0
        ),
    )(src, links)
    return total.reshape(1, 1, NYX, DOF, RHS)


def solution(mesh):
    placed = (P("ta", "gz", None, None, None), P("ta", "gz", None, None, None, None))
    return jax.shard_map(
        shards,
        mesh=mesh,
        in_specs=placed,
        out_specs=P("ta", "gz", None, None, None),
        check_vma=False,
    )
```

```python
import jax
import jax.numpy as jnp
from jax import lax
from jax.experimental import pallas as pl
from jax.experimental.pallas import tpu as pltpu
from jax.sharding import PartitionSpec as P

DOF = 96
DIRS = 9
RHS = 128
NX = 8
NY = 2
NYX = NX * NY
APPLIES = 4
CHUNK = 2
CHUNKS = NYX // CHUNK
STEPS = APPLIES * CHUNKS
DIRECT_EDGE = 5
DIRECT_NEAR = 6
DIRECT = 6
RELAY = CHUNKS
PASS = 5

FACES = 4
MESH = pl.DeviceIdType.MESH


def kernel(src, links_hbm, out, links, vecs, faces, relayed, load_sem, send_sem, recv_sem, relay_sem, pass_sem):
    t, z = lax.axis_index("ta"), lax.axis_index("gz")
    nt, nz = lax.axis_size("ta"), lax.axis_size("gz")
    half = nt // 2
    edge = lax.rem(t + 1, half) < 2
    off_edge = (lax.rem(t + 1, half) // 2 + half // 2 - 1) // (half // 2)
    near = jnp.logical_and(lax.rem(t + 2, half) < 4, jnp.logical_not(edge))
    inner = lax.rem(t + 2, half) >= 4
    high = t // half
    last = lax.rem(t, half) // (half // 2)

    z_out, z_out_face = lax.rem(z + high + (1 - high) * (nz - 1), nz), high
    z_over, z_over_face = lax.rem(z + (1 - high) + high * (nz - 1), nz), 1 - high
    t_in, t_in_face = lax.rem(t + (1 - last) + last * (nt - 1), nt), 3 - last
    t_over, t_over_face = lax.rem(t + last + (1 - last) * (nt - 1), nt), 2 + last
    own_edge = t + off_edge * (2 * last - 1)
    partner = lax.rem(own_edge + half, nt)
    partner_near = partner + 1 - 2 * last
    t_pass = lax.rem(own_edge + last + (1 - last) * (nt - 1) + half, nt)
    t_pass_near = t_pass - 1 + 2 * last

    load_links = pltpu.make_async_copy(links_hbm, links, load_sem.at[0])
    load_source = pltpu.make_async_copy(src, vecs.at[0], load_sem.at[1])
    load_source.start()
    load_links.start()

    barrier = pltpu.get_barrier_semaphore()

    def greet(target):
        pl.semaphore_signal(barrier, inc=1, device_id=target, device_id_type=MESH)

    greet((t, z_out))
    greet((t_in, z))
    greet((t, z_over))

    @pl.when(jnp.logical_not(inner))
    def _():
        greet((partner, z))
        greet((partner, z_out))
        greet((t_pass, z))

    @pl.when(edge)
    def _():
        greet((partner_near, z))
        greet((partner_near, z_out))
        greet((t_pass_near, z))
        pl.semaphore_wait(barrier, 9)

    @pl.when(near)
    def _():
        greet((t_over, z))
        pl.semaphore_wait(barrier, 7)

    @pl.when(inner)
    def _():
        greet((t_over, z))
        pl.semaphore_wait(barrier, 4)

    def remote(block, slot, send, recv, target):
        return pltpu.make_async_remote_copy(
            src_ref=block, dst_ref=slot, send_sem=send, recv_sem=recv, device_id=target, device_id_type=MESH
        )

    def part(c):
        return pl.ds(c * CHUNK, CHUNK)

    def push(block, k, c, face, target):
        remote(block, faces.at[k, face, part(c)], send_sem.at[k, face], recv_sem.at[k, face, c], target).start()

    def issue_relay(block, k, c):
        @pl.when(edge)
        def _():
            remote(
                block,
                relayed.at[k, part(c)],
                send_sem.at[k, z_over_face],
                relay_sem.at[k, c],
                (partner + lax.rem(c, 2) * (partner_near - partner), z),
            ).start()

    def issue_edge(block, k, c):
        @pl.when(edge)
        def _():
            push(block, k, c, z_out_face, (t, z_out))
            push(block, k, c, t_in_face, (t_in, z))

    def push_all(block, k, c):
        push(block, k, c, z_out_face, (t, z_out))
        push(block, k, c, z_over_face, (t, z_over))
        push(block, k, c, t_over_face, (t_over, z))
        push(block, k, c, t_in_face, (t_in, z))

    def issue_near(block, k, c):
        @pl.when(near)
        def _():
            push_all(block, k, c)

    def issue_inner(block, k, c):
        @pl.when(inner)
        def _():
            push_all(block, k, c)

    def passed(k, c):
        block = relayed.at[k, part(c)]
        on_z = remote(
            block, faces.at[k, z_out_face, part(c)], pass_sem.at[k, 0], recv_sem.at[k, z_out_face, c], (partner, z_out)
        )
        on_t = remote(
            block, faces.at[k, t_over_face, part(c)], pass_sem.at[k, 1], recv_sem.at[k, t_over_face, c], (t_pass, z)
        )
        return on_z, on_t

    def issue_pass(k, c):
        odd = lax.rem(c, 2) == 1

        @pl.when(jnp.logical_or(jnp.logical_and(edge, jnp.logical_not(odd)), jnp.logical_and(near, odd)))
        def _():
            remote(
                vecs.at[k, part(c)], relayed.at[k, part(c)], send_sem.at[k, 0], relay_sem.at[k, c], (partner, z)
            ).wait_recv()
            on_z, on_t = passed(k, c)
            on_z.start()
            on_t.start()

    def arrived(k, c):
        for face in range(FACES):
            remote(
                vecs.at[k, part(c)], faces.at[k, face, part(c)], send_sem.at[k, face], recv_sem.at[k, face, c], (t_in, z)
            ).wait_recv()

    def at_home(k, s):
        row, x = s // NX, lax.rem(s, NX)
        here = [
            s,
            row * NX + lax.rem(x + 1, NX),
            row * NX + lax.rem(x + NX - 1, NX),
            lax.rem(s + NX, NYX),
            lax.rem(s + NX, NYX),
        ]
        total = jnp.zeros((DOF, RHS), jnp.float32)
        for d, at in enumerate(here):
            total += jnp.dot(links[s, d], vecs[k, at], preferred_element_type=jnp.float32)
        return total

    def applied(k, c, store_site, send_ready):
        sites = [c * CHUNK + i for i in range(CHUNK)]
        totals = [at_home(k, s) for s in sites]
        arrived(k, c)
        send_ready()
        for s, total in zip(sites, totals):
            for face in range(FACES):
                total += jnp.dot(links[s, 5 + face], faces[k, face, s], preferred_element_type=jnp.float32)
            store_site(s, total)

    def whose(step):
        return step // CHUNKS, lax.rem(step, CHUNKS)

    def send(issue, step):
        k, c = whose(step)
        issue(vecs.at[k, part(c)], k, c)

    windows = [
        (issue_inner, DIRECT),
        (issue_near, DIRECT_NEAR),
        (issue_edge, DIRECT_EDGE),
    ]

    for c in range(CHUNKS):
        issue_relay(src.at[part(c)], 0, jnp.int32(c))
        for issue, ahead in windows:
            if c < ahead:
                issue(src.at[part(c)], 0, c)
        if c >= CHUNKS - PASS:
            issue_pass(0, jnp.int32(c - (CHUNKS - PASS)))
    load_source.wait()
    load_links.wait()

    @pl.loop(0, STEPS - CHUNKS)
    def _(step):
        k, c = whose(step)

        def keep(s, total):
            vecs[k + 1, s] = total.astype(jnp.bfloat16)

        def send_ready():
            for issue, ahead in windows:
                send(issue, step + ahead)

        applied(k, c, keep, send_ready)
        send(issue_relay, step + RELAY)
        issue_pass(*whose(step + PASS))

    def sent(k, sem, sites=NYX):
        block = pl.ds(0, sites)
        remote(vecs.at[k, block], faces.at[k, 0, block], sem, recv_sem.at[k, 0, 0], (t_in, z)).wait_send()

    def sent_round(k):
        sent(k, send_sem.at[k, z_out_face])
        sent(k, send_sem.at[k, z_over_face])
        sent(k, send_sem.at[k, t_in_face])

        @pl.when(jnp.logical_not(inner))
        def _():
            sent(k, pass_sem.at[k, 0], NYX // 2)
            sent(k, pass_sem.at[k, 1], NYX // 2)

        @pl.when(jnp.logical_not(edge))
        def _():
            sent(k, send_sem.at[k, t_over_face])

    for k in range(APPLIES - 2):
        sent_round(k)

    @pl.loop(0, CHUNKS)
    def _(c):
        def keep(s, total):
            out[s] = total

        def send_ready():
            for issue, ahead in windows:

                @pl.when(c + ahead < CHUNKS)
                def _():
                    send(issue, STEPS - CHUNKS + c + ahead)

        applied(APPLIES - 1, c, keep, send_ready)

        @pl.when(c + PASS < CHUNKS)
        def _():
            issue_pass(APPLIES - 1, c + PASS)


    sent_round(APPLIES - 2)
    sent_round(APPLIES - 1)


def shards(source, link_blocks):
    src = pltpu.with_memory_space_constraint(source.reshape(NYX, DOF, RHS), pltpu.HBM)
    links = pltpu.with_memory_space_constraint(link_blocks.reshape(NYX, DIRS, DOF, DOF), pltpu.HBM)
    total = pl.pallas_call(
        kernel,
        out_shape=pltpu.VMEM((NYX, DOF, RHS), jnp.float32),
        in_specs=[pl.BlockSpec(memory_space=pl.ANY)] * 2,
        out_specs=pl.BlockSpec(memory_space=pltpu.VMEM),
        scratch_shapes=[
            pltpu.VMEM((NYX, DIRS, DOF, DOF), jnp.bfloat16),
            pltpu.VMEM((APPLIES, NYX, DOF, RHS), jnp.bfloat16),
            pltpu.VMEM((APPLIES, FACES, NYX, DOF, RHS), jnp.bfloat16),
            pltpu.VMEM((APPLIES, NYX, DOF, RHS), jnp.bfloat16),
            pltpu.SemaphoreType.DMA((2,)),
            pltpu.SemaphoreType.DMA((APPLIES, FACES)),
            pltpu.SemaphoreType.DMA((APPLIES, FACES, CHUNKS)),
            pltpu.SemaphoreType.DMA((APPLIES, CHUNKS)),
            pltpu.SemaphoreType.DMA((APPLIES, 2)),
        ],
        compiler_params=pltpu.CompilerParams(
            collective_id=0, has_side_effects=True, vmem_limit_bytes=40 * 2**20
        ),
        cost_estimate=pl.CostEstimate(
            flops=2 * APPLIES * NYX * DIRS * DOF * DOF * RHS, bytes_accessed=6 * 2**20, transcendentals=0
        ),
    )(src, links)
    return total.reshape(1, 1, NYX, DOF, RHS)


def solution(mesh):
    placed = (P("ta", "gz", None, None, None), P("ta", "gz", None, None, None, None))
    return jax.shard_map(
        shards,
        mesh=mesh,
        in_specs=placed,
        out_specs=P("ta", "gz", None, None, None),
        check_vma=False,
    )
```
